512 devices in a mesh: gx: 64 (over x, y, z_hi), gy: 8 (over z_lo, core).
Axes of the slice: x: 4, y: 8, z: 8 (z_hi: 2, z_lo: 4; z = z_hi * 4 + z_lo), core: 2. Of those that a mesh axis runs over, the one named last changes fastest.
Arguments:
- displacement: float32 [3, 128, 256, 256], P(None, 'gx', 'gy'), may hold values from -6 to 6
- load: float32 [3, 128, 256, 256], P(None, 'gx', 'gy'), may hold values from -120 to 120
- element_phase: int32 [128, 256, 256], P('gx', 'gy'), may hold values from 0 to 2
- element_modulus: float32 [128, 256, 256], P('gx', 'gy'), may hold values from 1 to 10
- stiffness: float32 [3, 8, 8, 3, 3], replicated, as said below
Outputs:
- relaxed: float32 [3, 128, 256, 256], P(None, 'gx', 'gy')
The draws below stay inside these ranges and needn't reach their ends.
Inputs may be any that keep to these rules, and one draw needn't show every extreme that they name: For every phase and corner c, stiffness[ph, c, c] has diagonal entries between 2 and 3 and other entries of magnitude at most 0.3.
All inputs are finite; a program needn't handle non-finite values.
Results may differ from the reference program's by a relative error of at most 0.0001.
Values sent between devices are 32-bit elements; how exact they have to be, the bound alone decides.
No kernel may reach another device: no remote copies, remote signals or barrier semaphores. Data moves between devices by JAX's collectives and lax.ppermute only.
A program may use at most 64 MiB of HBM per device.

```python
import math
import jax
import jax.numpy as jnp
from jax import lax

NZ = 256
PHASES = 3
NX = 128
NY = 256


def draw_stiffness(key, part):
    key = jax.random.fold_in(key, 11)
    key_far, key_near, key_main = jax.random.split(key, 3)
    shape = (PHASES, 8, 8, 3, 3)
    coupled = jax.random.normal(key_far, shape, jnp.float32) * 0.6
    near = jax.random.uniform(key_near, shape, jnp.float32, -0.3, 0.3)
    main = jax.random.uniform(key_main, shape, jnp.float32, 2.0, 3.0)
    identity = jnp.eye(3, dtype=jnp.float32)
    same_corner = jnp.eye(8, dtype=jnp.float32)[None, :, :, None, None]
    inner = identity * main + (1.0 - identity) * near
    return same_corner * inner + (1.0 - same_corner) * coupled


def touch_ends(result, rng, least, high):
    extent = result.shape
    spot = [jax.random.randint(jax.random.fold_in(rng, axis), (), 0, extent[axis]) for axis in range(len(extent))]
    result = result.at[tuple(spot)].set(least)
    longest = extent.index(max(extent))
    spot[longest] = (spot[longest] + 1) % extent[longest]
    return result.at[tuple(spot)].set(high)


def block_scale(rng, shape, cuts, least, high):
    gain, own = 1.0, jax.random.fold_in(rng, 6)
    for dim, blocks in cuts:
        draws = jnp.exp(jax.random.uniform(jax.random.fold_in(own, dim), (blocks,), jnp.float32, least / len(cuts), high / len(cuts)))
        gain = gain * jnp.repeat(draws, shape[dim] // blocks).reshape([-1 if axis == dim else 1 for axis in range(len(shape))])
    return gain


def normal_values(rng, dims, deviation, most, shards=(), kind=jnp.bfloat16):
    values = jax.random.normal(rng, dims, jnp.float32) * deviation
    if len(shards) > 0:
        values = block_scale(rng, dims, shards, -0.22, 0.18) * values
    return jnp.clip(values, min=-most, max=most).astype(kind)


def setup_inputs(seed: int = 0) -> dict:
    seeds = jax.random.split(jax.random.key(seed), 6)
    displacement = normal_values(seeds[0], (3, NX, NY, NZ), 1.0, 6.0, ((1, 64), (2, 8)), jnp.float32)
    load = normal_values(seeds[1], (3, NX, NY, NZ), 20.0, 120.0, ((1, 64), (2, 8)), jnp.float32)
    element_phase = touch_ends(jax.random.randint(seeds[2], (NX, NY, NZ), 0, PHASES), jax.random.fold_in(seeds[2], 1), 0, PHASES - 1).astype(jnp.int32)
    element_modulus = jnp.clip(jnp.exp(math.log(10.0) - 2.3025851 * jax.random.uniform(seeds[3], (NX, NY, NZ), jnp.float32) ** block_scale(seeds[3], (NX, NY, NZ), ((0, 64), (1, 8)), -0.2, 0.2)), 1.0, 10.0)
    stiffness = draw_stiffness(jax.random.fold_in(seeds[5], 71), 0)
    return dict(displacement=displacement, load=load, element_phase=element_phase, element_modulus=element_modulus, stiffness=stiffness)


corner_list = tuple((first, second, third) for first in (0, 1) for second in (0, 1) for third in (0, 1))


def pick_strided(array, offset, parity, counts):
    starts = (0,) + tuple(bit + step + 1 for bit, step in zip(parity, offset))
    limits = (array.shape[0],) + tuple(begin + 2 * (count - 1) + 1 for begin, count in zip(starts[1:], counts))
    return lax.slice(array, starts, limits, (1, 2, 2, 2))


def solve_blocks(matrix, right):
    m00, m01, m02 = matrix[0, 0], matrix[0, 1], matrix[0, 2]
    m10, m11, m12 = matrix[1, 0], matrix[1, 1], matrix[1, 2]
    m20, m21, m22 = matrix[2, 0], matrix[2, 1], matrix[2, 2]
    c00 = m11 * m22 - m12 * m21
    c01 = m12 * m20 - m10 * m22
    c02 = m10 * m21 - m11 * m20
    c10 = m02 * m21 - m01 * m22
    c11 = m00 * m22 - m02 * m20
    c12 = m01 * m20 - m00 * m21
    c20 = m01 * m12 - m02 * m11
    c21 = m02 * m10 - m00 * m12
    c22 = m00 * m11 - m01 * m10
    determinant = m00 * c00 + m01 * c01 + m02 * c02
    first = (c00 * right[0] + c10 * right[1] + c20 * right[2]) / determinant
    second = (c01 * right[0] + c11 * right[1] + c21 * right[2]) / determinant
    third = (c02 * right[0] + c12 * right[1] + c22 * right[2]) / determinant
    return jnp.stack([first, second, third], axis=0)


def colour_update(disp_ext, weight_ext, load_sel, stiffness, parity):
    counts = load_sel.shape[1:]
    accum = jnp.zeros(load_sel.shape, load_sel.dtype)
    diagonal = jnp.zeros((3, 3) + counts, load_sel.dtype)
    for corner_index, corner in enumerate(corner_list):
        backward = tuple(-entry for entry in corner)
        weight_sel = pick_strided(weight_ext, backward, parity, counts)
        for partner_index, partner in enumerate(corner_list):
            table = stiffness[:, corner_index, partner_index][:, :, :, None, None, None]
            coupling = jnp.sum(weight_sel[:, None, None] * table, axis=0)
            if partner_index == corner_index:
                diagonal = diagonal + coupling
            else:
                offset = tuple(later - earlier for later, earlier in zip(partner, corner))
                neighbour = pick_strided(disp_ext, offset, parity, counts)
                accum = accum + jnp.sum(coupling * neighbour[None], axis=1)
    return solve_blocks(diagonal, load_sel - accum)


def reference(displacement, load, element_phase, element_modulus, stiffness):
    phase_ids = jnp.arange(stiffness.shape[0], dtype=jnp.int32)
    weights = jnp.where(element_phase[None] == phase_ids[:, None, None, None], element_modulus[None], jnp.zeros_like(element_modulus)[None])
    padding = ((0, 0), (1, 1), (1, 1), (1, 1))
    weight_ext = jnp.pad(weights, padding, mode="wrap")
    current = displacement
    for parity in ((0, 0, 0), (1, 0, 0)):
        disp_ext = jnp.pad(current, padding, mode="wrap")
        load_sel = load[:, parity[0]::2, parity[1]::2, parity[2]::2]
        fresh = colour_update(disp_ext, weight_ext, load_sel, stiffness, parity)
        current = current.at[:, parity[0]::2, parity[1]::2, parity[2]::2].set(fresh)
    return current
```

```python
import jax
import jax.numpy as jnp
from jax import lax
from jax.experimental import pallas as pl
from jax.experimental.pallas import tpu as pltpu
from jax.sharding import PartitionSpec as P

PARITY = {"0": (0, 0), "1": (1, 1), "s": (0, 1), "o": (1, 0)}


def shifted(x, axis, by):
    devices = lax.axis_size(axis)
    return lax.ppermute(x, axis, [(i, (i + by) % devices) for i in range(devices)])


def tiles(a):
    rows, cols = a.shape
    return jnp.stack(
        [a[r : r + 8, c : c + 128] for r in range(0, rows, 8) for c in range(0, cols, 128)]
    )


def flat(t, cols):
    across = cols // 128
    rows = [
        jnp.concatenate([t[r + c] for c in range(across)], axis=1)
        for r in range(0, t.shape[0], across)
    ]
    return jnp.concatenate(rows, axis=0)


def even_lanes(shape):
    return lax.broadcasted_iota(jnp.int32, shape, len(shape) - 1) % 2 == 0


def next_lane(a):
    return pltpu.roll(a, a.shape[-1] - 1, a.ndim - 1)


def last_lane(a):
    return pltpu.roll(a, 1, a.ndim - 1)


def down_row(a, top):
    first = lax.broadcasted_iota(jnp.int32, a.shape, 0) == 0
    return jnp.where(first, jnp.broadcast_to(top, a.shape), pltpu.roll(a, 1, 0))


def pair_even(a):
    here, there = tiles(a), tiles(next_lane(a))
    even = even_lanes((8, 128))[None]
    return {"s": jnp.where(even, here, there), "o": jnp.where(even, there, here)}


def pair_odd(a):
    return {"0": tiles(a), "1": tiles(next_lane(a))}


def plane_views(even_rows, odd_rows, tops):
    same = [pair_even(a) for a in even_rows]
    after = [pair_odd(a) for a in odd_rows]
    before = [pair_odd(down_row(a, top)) for a, top in zip(odd_rows, tops)]
    return same, after, before


class Elements:
    def __init__(self, modulus, phase):
        self.modulus = tiles(modulus)
        self.phase = tiles(phase)


class Summer:
    def __init__(self, table):
        self.table = table
        self.even = even_lanes((8, 128))
        self.corners = 8

    def entry(self, elements, corner, partner, kind, i, j):
        first, second = PARITY[kind]
        picked = []
        for ph in range(3):
            places = []
            for parity, side in ((0, first), (1, second)):
                c = corner * 2 + parity
                d = partner * 2 + side
                places.append(self.table[(((ph * 8 + c) * 8 + d) * 3 + i) * 3 + j])
            picked.append(jnp.where(self.even, places[0], places[1])[None])
        return jnp.where(
            elements.phase == 0, picked[0], jnp.where(elements.phase == 1, picked[1], picked[2])
        )

    def force(self, elements, corner, terms):
        total = [None] * 3
        for partner, kind, values in terms:
            for i in range(3):
                for j in range(3):
                    part = self.entry(elements, corner, partner, kind, i, j) * values[j]
                    total[i] = part if total[i] is None else total[i] + part
        return [elements.modulus * part for part in total]

    def diagonal(self, elements, corner):
        return [
            elements.modulus * self.entry(elements, corner, corner, "s", i, j)
            for i in range(3)
            for j in range(3)
        ]


def pick(views, kind):
    return [view[kind] for view in views]


def terms_of(views, cx, cy, dx, kinds):
    same, after, before = views
    other = after if cy == 0 else before
    found = [(dx * 2 + cy, kind, pick(same, kind)) for kind in kinds]
    found += [(dx * 2 + 1 - cy, kind, pick(other, kind)) for kind in ("0", "1")]
    return found


def added(left, right):
    return [a + b for a, b in zip(left, right)]


def at_nodes(parts, cols):
    out = []
    for part in parts:
        whole = flat(part, cols)
        out.append(whole + last_lane(whole))
    return out


def inverse_of(m):
    m00, m01, m02, m10, m11, m12, m20, m21, m22 = m
    c00 = m11 * m22 - m12 * m21
    c01 = m12 * m20 - m10 * m22
    c02 = m10 * m21 - m11 * m20
    c10 = m02 * m21 - m01 * m22
    c11 = m00 * m22 - m02 * m20
    c12 = m01 * m20 - m00 * m21
    c20 = m01 * m12 - m02 * m11
    c21 = m02 * m10 - m00 * m12
    c22 = m00 * m11 - m01 * m10
    determinant = m00 * c00 + m01 * c01 + m02 * c02
    scale = 1.0 / determinant
    return [a * scale for a in (c00, c10, c20, c01, c11, c21, c02, c12, c22)]


def applied(inverse, right):
    return [sum(inverse[3 * i + j] * right[j] for j in range(3)) for i in range(3)]


class Rows:
    def __init__(self, work_ref):
        self.work, self.slot = work_ref, 0

    def split(self, a):
        parts, slot, half = a.shape[1] // 128, self.slot, a.shape[0] // 2
        self.slot += 1
        for k in range(parts):
            self.work[slot, k] = a[:, k * 128 : (k + 1) * 128]
        return tuple(
            jnp.concatenate([self.work[slot, k, pl.ds(bit, half, 2), :] for k in range(parts)], axis=1)
            for bit in range(2)
        )

    def merge(self, even, odd):
        parts, slot, half = even.shape[1] // 128, self.slot, even.shape[0]
        self.slot += 1
        for k in range(parts):
            self.work[slot, k, pl.ds(0, half, 2), :] = even[:, k * 128 : (k + 1) * 128]
            self.work[slot, k, pl.ds(1, half, 2), :] = odd[:, k * 128 : (k + 1) * 128]
        return jnp.concatenate([self.work[slot, k] for k in range(parts)], axis=1)


def local_plane(rows, u_ref, halo_ref, plane):
    split = [rows.split(u_ref[c, plane]) for c in range(3)]
    even, odd = [a for a, _ in split], [b for _, b in split]
    tops = [halo_ref[3 * plane + c : 3 * plane + c + 1, :] for c in range(3)]
    return even, odd, tops


def element_rows(rows, mod_ref, phase_ref, halo_ref, plane):
    split = [rows.split(mod_ref[plane]), rows.split(phase_ref[plane].astype(jnp.float32))]
    even, odd = [a for a, _ in split], [b for _, b in split]
    before = (
        down_row(odd[0], halo_ref[6 + plane : 7 + plane, :]),
        down_row(odd[1], halo_ref[8 + plane : 9 + plane, :]),
    )
    return even, before


def rim_kernel(u_ref, mod_ref, phase_ref, out_ref):
    out_ref[...] = jnp.zeros(out_ref.shape, jnp.float32)
    for plane in range(2):
        for c in range(3):
            out_ref[3 * plane + c : 3 * plane + c + 1, :] = u_ref[c, plane, 7:8, :]
        out_ref[6 + plane : 7 + plane, :] = mod_ref[plane, 7:8, :]
        out_ref[8 + plane : 9 + plane, :] = phase_ref[plane, 7:8, :].astype(jnp.float32)


def pack_kernel(table, u_ref, load_ref, mod_ref, phase_ref, halo_ref, back_ref, ahead_ref, work_ref):
    half, cols = u_ref.shape[2] // 2, u_ref.shape[3]
    quarter = half // 2
    summer, rows = Summer(table), Rows(work_ref)
    even_zero, odd_zero, top_zero = local_plane(rows, u_ref, halo_ref, 0)
    even_one, odd_one, top_one = local_plane(rows, u_ref, halo_ref, 1)
    zero = plane_views(even_zero, odd_zero, top_zero)
    one = plane_views(even_one, odd_one, top_one)
    rows_zero = element_rows(rows, mod_ref, phase_ref, halo_ref, 0)
    rows_one = element_rows(rows, mod_ref, phase_ref, halo_ref, 1)
    even = even_lanes((half, cols))
    own, beyond = None, None
    for cy in range(2):
        elements = Elements(*rows_zero[cy])
        part = summer.force(
            elements, cy, terms_of(zero, 0, cy, 0, "o") + terms_of(one, 0, cy, 1, "so")
        )
        own = part if own is None else added(own, part)
        elements = Elements(*rows_one[cy])
        part = summer.force(elements, 2 + cy, terms_of(one, 1, cy, 0, "so"))
        beyond = part if beyond is None else added(beyond, part)
    own = at_nodes(own, cols)
    beyond = at_nodes(beyond, cols)
    back_ref[160:168, :] = jnp.zeros((8, cols), jnp.float32)
    for c in range(3):
        left = rows.split(load_ref[c, 0])[0] - own[c]
        back_ref[c * half : (c + 1) * half, :] = jnp.where(even, left, even_zero[c])
        back_ref[(3 + c) * half : (4 + c) * half, :] = odd_zero[c]
        back_ref[10 * half + c : 10 * half + c + 1, :] = top_zero[c]
    for cy in range(2):
        for k in range(2):
            back_ref[(6 + 2 * k + cy) * half : (7 + 2 * k + cy) * half, :] = rows_zero[cy][k]
            start = half + quarter + (2 * k + cy) * half
            ahead_ref[start : start + half, :] = rows_one[cy][k]
    ahead_ref[0:half, :] = jnp.where(even, beyond[0], last_lane(beyond[1]))
    ahead_ref[half : half + quarter, :] = jnp.where(
        even[:quarter], beyond[2][:quarter], last_lane(beyond[2][quarter:])
    )


def inner_kernel(table, u_ref, load_ref, mod_ref, phase_ref, halo_ref, sums_ref, work_ref):
    half, cols = u_ref.shape[2] // 2, u_ref.shape[3]
    summer, rows = Summer(table), Rows(work_ref)
    zero = plane_views(*local_plane(rows, u_ref, halo_ref, 0))
    one = plane_views(*local_plane(rows, u_ref, halo_ref, 1))
    rows_zero = element_rows(rows, mod_ref, phase_ref, halo_ref, 0)
    rows_one = element_rows(rows, mod_ref, phase_ref, halo_ref, 1)
    total, middle, first, last = None, None, None, None
    for cy in range(2):
        left, right = Elements(*rows_zero[cy]), Elements(*rows_one[cy])
        part = summer.force(left, 2 + cy, terms_of(zero, 1, cy, 0, "o") + terms_of(one, 1, cy, 1, "o"))
        part = added(part, summer.force(right, cy, terms_of(one, 0, cy, 0, "o")))
        total = part if total is None else added(total, part)
        near = summer.diagonal(left, cy)
        mid = added(summer.diagonal(left, 2 + cy), summer.diagonal(right, cy))
        far = summer.diagonal(right, 2 + cy)
        first = near if first is None else added(first, near)
        middle = mid if middle is None else added(middle, mid)
        last = far if last is None else added(last, far)
    total = at_nodes(total, cols)
    for c in range(3):
        sums_ref[c] = rows.split(load_ref[c, 1])[0] - total[c]
    solved = inverse_of(at_nodes(middle, cols))
    first = at_nodes(first, cols)
    last = at_nodes(last, cols)
    for k in range(9):
        sums_ref[3 + k] = solved[k]
        sums_ref[12 + k] = first[k]
        sums_ref[21 + k] = last[k]


def unpacked(ref, half):
    quarter = half // 2
    block = ref[0:half, :]
    rest = ref[half : half + quarter, :]
    return [block, next_lane(block), jnp.concatenate([rest, next_lane(rest)], axis=0)]


def finish_kernel(
    table, u_ref, mod_ref, phase_ref, halo_ref, sums_ref, mine_back, mine_ahead, back_ref, ahead_ref, out_ref, work_ref
):
    half, cols = u_ref.shape[2] // 2, u_ref.shape[3]
    quarter = half // 2
    summer, rows = Summer(table), Rows(work_ref)
    even_zero, odd_zero, top_zero = local_plane(rows, u_ref, halo_ref, 0)
    zero = plane_views(even_zero, odd_zero, top_zero)
    rows_zero = element_rows(rows, mod_ref, phase_ref, halo_ref, 0)
    rows_one = element_rows(rows, mod_ref, phase_ref, halo_ref, 1)
    even_two = [back_ref[c * half : (c + 1) * half, :] for c in range(3)]
    odd_two = [back_ref[(3 + c) * half : (4 + c) * half, :] for c in range(3)]
    top_two = [back_ref[10 * half + c : 10 * half + c + 1, :] for c in range(3)]
    two = plane_views(even_two, odd_two, top_two)
    even = even_lanes((half, cols))
    before, after, lower, upper, beyond = None, None, None, None, None
    for cy in range(2):
        start = half + quarter + cy * half
        minus = Elements(ahead_ref[start : start + half, :], ahead_ref[start + 2 * half : start + 3 * half, :])
        start = (6 + cy) * half
        plus = Elements(back_ref[start : start + half, :], back_ref[start + 2 * half : start + 3 * half, :])
        right = Elements(*rows_one[cy])
        part = summer.force(minus, 2 + cy, terms_of(zero, 1, cy, 1, "o"))
        before = part if before is None else added(before, part)
        part = summer.force(right, 2 + cy, terms_of(two, 1, cy, 1, "o"))
        after = part if after is None else added(after, part)
        part = summer.force(right, cy, terms_of(two, 0, cy, 1, "o"))
        beyond = part if beyond is None else added(beyond, part)
        part = summer.diagonal(minus, 2 + cy)
        lower = part if lower is None else added(lower, part)
        part = summer.diagonal(plus, cy)
        upper = part if upper is None else added(upper, part)
    before, after = at_nodes(before, cols), at_nodes(after, cols)
    lower, upper = at_nodes(lower, cols), at_nodes(upper, cols)
    came, sent = unpacked(ahead_ref, half), unpacked(mine_ahead, half)
    right = [mine_back[c * half : (c + 1) * half, :] - came[c] - before[c] for c in range(3)]
    first_new = applied(inverse_of([sums_ref[12 + k] + lower[k] for k in range(9)]), right)
    right = [even_two[c] - sent[c] - after[c] for c in range(3)]
    third_new = applied(inverse_of([sums_ref[21 + k] + upper[k] for k in range(9)]), right)
    near = [pair_even(a)["s"] for a in first_new]
    far = [pair_even(a)["s"] for a in third_new]
    for cy in range(2):
        left, right = Elements(*rows_zero[cy]), Elements(*rows_one[cy])
        beyond = added(beyond, summer.force(left, 2 + cy, [(cy, "s", near)]))
        beyond = added(beyond, summer.force(right, cy, [(2 + cy, "s", far)]))
    beyond = at_nodes(beyond, cols)
    solved = [sums_ref[3 + k] for k in range(9)]
    second_new = applied(solved, [sums_ref[c] - beyond[c] for c in range(3)])
    for c in range(3):
        out_ref[c, 0] = rows.merge(jnp.where(even, first_new[c], even_zero[c]), odd_zero[c])
        own, other = rows.split(u_ref[c, 1])
        out_ref[c, 1] = rows.merge(jnp.where(even, second_new[c], own), other)


def whole():
    return pl.BlockSpec(memory_space=pltpu.VMEM)


def scalars():
    return pl.BlockSpec(memory_space=pltpu.SMEM)


def on_device(displacement, load, element_phase, element_modulus, stiffness):
    planes, rows, cols = displacement.shape[1:]
    half = rows // 2
    kind = displacement.dtype
    table = stiffness.reshape(-1)
    last = rows // 8 - 1
    slots = 16
    rim = pl.pallas_call(
        rim_kernel,
        grid=(1,),
        in_specs=[
            pl.BlockSpec((3, planes, 8, cols), lambda i: (0, 0, last, 0)),
            pl.BlockSpec((planes, 8, cols), lambda i: (0, last, 0)),
            pl.BlockSpec((planes, 8, cols), lambda i: (0, last, 0)),
        ],
        out_specs=pl.BlockSpec((16, cols), lambda i: (0, 0)),
        out_shape=jax.ShapeDtypeStruct((16, cols), kind),
    )(displacement, element_modulus, element_phase)
    halo = shifted(rim, "gy", 1)
    back_rows, ahead_rows = 10 * half + 8, 5 * half + half // 2
    back, ahead = pl.pallas_call(
        pack_kernel,
        in_specs=[scalars()] + [whole()] * 5,
        out_specs=[whole()] * 2,
        out_shape=[
            jax.ShapeDtypeStruct((back_rows, cols), kind),
            jax.ShapeDtypeStruct((ahead_rows, cols), kind),
        ],
        scratch_shapes=[pltpu.VMEM((slots, cols // 128, rows, 128), kind)],
        compiler_params=pltpu.CompilerParams(vmem_limit_bytes=24 << 20),
    )(table, displacement, load, element_modulus, element_phase, halo)
    from_next = shifted(back, "gx", -1)
    from_last = shifted(ahead, "gx", 1)
    sums = pl.pallas_call(
        inner_kernel,
        in_specs=[scalars()] + [whole()] * 5,
        out_specs=whole(),
        out_shape=jax.ShapeDtypeStruct((30, half, cols), kind),
        scratch_shapes=[pltpu.VMEM((slots, cols // 128, rows, 128), kind)],
        compiler_params=pltpu.CompilerParams(vmem_limit_bytes=24 << 20),
        cost_estimate=pl.CostEstimate(flops=20_000_000, bytes_accessed=1_000_000, transcendentals=0),
    )(table, displacement, load, element_modulus, element_phase, halo)
    return pl.pallas_call(
        finish_kernel,
        in_specs=[scalars()] + [whole()] * 9,
        out_specs=whole(),
        out_shape=jax.ShapeDtypeStruct(displacement.shape, kind),
        scratch_shapes=[pltpu.VMEM((slots, cols // 128, rows, 128), kind)],
        compiler_params=pltpu.CompilerParams(vmem_limit_bytes=24 << 20),
    )(
        table, displacement, element_modulus, element_phase, halo, sums, back, ahead, from_next, from_last
    )


def solution(mesh):
    in_specs = (
        P(None, "gx", "gy", None),
        P(None, "gx", "gy", None),
        P("gx", "gy", None),
        P("gx", "gy", None),
        P(),
    )
    out_specs = P(None, "gx", "gy", None)
    return jax.shard_map(
        on_device, mesh=mesh, in_specs=in_specs, out_specs=out_specs, check_vma=False
    )
```

```python
import jax
import jax.numpy as jnp
from jax import lax
from jax.experimental import pallas as pl
from jax.experimental.pallas import tpu as pltpu
from jax.sharding import PartitionSpec as P

PARITY = {"0": (0, 0), "1": (1, 1), "s": (0, 1), "o": (1, 0)}


def shifted(x, axis, by):
    devices = lax.axis_size(axis)
    return lax.ppermute(x, axis, [(i, (i + by) % devices) for i in range(devices)])


def shifted_from(x, axis, by, parity):
    devices = lax.axis_size(axis)
    return lax.ppermute(x, axis, [(i, (i + by) % devices) for i in range(parity, devices, 2)])


def tiles(a):
    rows, cols = a.shape
    return jnp.stack(
        [a[r : r + 8, c : c + 128] for r in range(0, rows, 8) for c in range(0, cols, 128)]
    )


def flat(t, cols):
    across = cols // 128
    rows = [
        jnp.concatenate([t[r + c] for c in range(across)], axis=1)
        for r in range(0, t.shape[0], across)
    ]
    return jnp.concatenate(rows, axis=0)


def even_lanes(shape):
    return lax.broadcasted_iota(jnp.int32, shape, len(shape) - 1) % 2 == 0


def next_lane(a):
    return pltpu.roll(a, a.shape[-1] - 1, a.ndim - 1)


def last_lane(a):
    return pltpu.roll(a, 1, a.ndim - 1)


def down_row(a, top):
    first = lax.broadcasted_iota(jnp.int32, a.shape, 0) == 0
    return jnp.where(first, jnp.broadcast_to(top, a.shape), pltpu.roll(a, 1, 0))


def pair_even(a):
    here, there = tiles(a), tiles(next_lane(a))
    even = even_lanes((8, 128))[None]
    return {"s": jnp.where(even, here, there), "o": jnp.where(even, there, here)}


def pair_odd(a):
    return {"0": tiles(a), "1": tiles(next_lane(a))}


def plane_views(even_rows, odd_rows, tops):
    same = [pair_even(a) for a in even_rows]
    after = [pair_odd(a) for a in odd_rows]
    before = [pair_odd(down_row(a, top)) for a, top in zip(odd_rows, tops)]
    return same, after, before


class Elements:
    def __init__(self, modulus, phase):
        self.modulus = tiles(modulus)
        self.phase = tiles(phase)


class Summer:
    def __init__(self, table):
        self.table = table
        self.even = even_lanes((8, 128))
        self.corners = 8

    def entry(self, elements, corner, partner, kind, i, j):
        first, second = PARITY[kind]
        picked = []
        for ph in range(3):
            places = []
            for parity, side in ((0, first), (1, second)):
                c = corner * 2 + parity
                d = partner * 2 + side
                places.append(self.table[(((ph * 8 + c) * 8 + d) * 3 + i) * 3 + j])
            picked.append(jnp.where(self.even, places[0], places[1])[None])
        return jnp.where(
            elements.phase == 0, picked[0], jnp.where(elements.phase == 1, picked[1], picked[2])
        )

    def force(self, elements, corner, terms):
        total = [None] * 3
        for partner, kind, values in terms:
            for i in range(3):
                for j in range(3):
                    part = self.entry(elements, corner, partner, kind, i, j) * values[j]
                    total[i] = part if total[i] is None else total[i] + part
        return [elements.modulus * part for part in total]

    def diagonal(self, elements, corner):
        return [
            elements.modulus * self.entry(elements, corner, corner, "s", i, j)
            for i in range(3)
            for j in range(3)
        ]


def pick(views, kind):
    return [view[kind] for view in views]


def terms_of(views, cx, cy, dx, kinds):
    same, after, before = views
    other = after if cy == 0 else before
    found = [(dx * 2 + cy, kind, pick(same, kind)) for kind in kinds]
    found += [(dx * 2 + 1 - cy, kind, pick(other, kind)) for kind in ("0", "1")]
    return found


def added(left, right):
    return [a + b for a, b in zip(left, right)]


def at_nodes(parts, cols):
    out = []
    for part in parts:
        whole = flat(part, cols)
        out.append(whole + last_lane(whole))
    return out


def inverse_of(m):
    m00, m01, m02, m10, m11, m12, m20, m21, m22 = m
    c00 = m11 * m22 - m12 * m21
    c01 = m12 * m20 - m10 * m22
    c02 = m10 * m21 - m11 * m20
    c10 = m02 * m21 - m01 * m22
    c11 = m00 * m22 - m02 * m20
    c12 = m01 * m20 - m00 * m21
    c20 = m01 * m12 - m02 * m11
    c21 = m02 * m10 - m00 * m12
    c22 = m00 * m11 - m01 * m10
    determinant = m00 * c00 + m01 * c01 + m02 * c02
    scale = 1.0 / determinant
    return [a * scale for a in (c00, c10, c20, c01, c11, c21, c02, c12, c22)]


def applied(inverse, right):
    return [sum(inverse[3 * i + j] * right[j] for j in range(3)) for i in range(3)]


class Rows:
    def __init__(self, work_ref):
        self.work, self.slot = work_ref, 0

    def split(self, a):
        parts, slot, half = a.shape[1] // 128, self.slot, a.shape[0] // 2
        self.slot += 1
        for k in range(parts):
            self.work[slot, k] = a[:, k * 128 : (k + 1) * 128]
        return tuple(
            jnp.concatenate([self.work[slot, k, pl.ds(bit, half, 2), :] for k in range(parts)], axis=1)
            for bit in range(2)
        )

    def merge(self, even, odd):
        parts, slot, half = even.shape[1] // 128, self.slot, even.shape[0]
        self.slot += 1
        for k in range(parts):
            self.work[slot, k, pl.ds(0, half, 2), :] = even[:, k * 128 : (k + 1) * 128]
            self.work[slot, k, pl.ds(1, half, 2), :] = odd[:, k * 128 : (k + 1) * 128]
        return jnp.concatenate([self.work[slot, k] for k in range(parts)], axis=1)


def local_plane(rows, u_ref, halo_ref, plane):
    split = [rows.split(u_ref[c, plane]) for c in range(3)]
    even, odd = [a for a, _ in split], [b for _, b in split]
    tops = [halo_ref[3 * plane + c : 3 * plane + c + 1, :] for c in range(3)]
    return even, odd, tops


def element_rows(rows, mod_ref, phase_ref, halo_ref, plane):
    split = [rows.split(mod_ref[plane]), rows.split(phase_ref[plane].astype(jnp.float32))]
    even, odd = [a for a, _ in split], [b for _, b in split]
    before = (
        down_row(odd[0], halo_ref[6 + plane : 7 + plane, :]),
        down_row(odd[1], halo_ref[8 + plane : 9 + plane, :]),
    )
    return even, before


def rim_kernel(u_ref, mod_ref, phase_ref, out_ref):
    out_ref[...] = jnp.zeros(out_ref.shape, jnp.float32)
    for plane in range(2):
        for c in range(3):
            out_ref[3 * plane + c : 3 * plane + c + 1, :] = u_ref[c, plane, 7:8, :]
        out_ref[6 + plane : 7 + plane, :] = mod_ref[plane, 7:8, :]
        out_ref[8 + plane : 9 + plane, :] = phase_ref[plane, 7:8, :].astype(jnp.float32)


def ahead_kernel(table, u_ref, mod_ref, phase_ref, halo_ref, back_ref, ahead_ref, top_ref, end_ref, work_ref):
    half, cols = u_ref.shape[2] // 2, u_ref.shape[3]
    quarter = half // 2
    summer, rows = Summer(table), Rows(work_ref)
    top_ref[...] = back_ref[: top_ref.shape[0], :]
    end_ref[...] = back_ref[top_ref.shape[0] :, :]
    one = plane_views(*local_plane(rows, u_ref, halo_ref, 1))
    rows_one = element_rows(rows, mod_ref, phase_ref, halo_ref, 1)
    even = even_lanes((half, cols))
    beyond = None
    for cy in range(2):
        elements = Elements(*rows_one[cy])
        part = summer.force(elements, 2 + cy, terms_of(one, 1, cy, 0, "so"))
        beyond = part if beyond is None else added(beyond, part)
        for k in range(2):
            start = half + quarter + (2 * k + cy) * half
            ahead_ref[start : start + half, :] = rows_one[cy][k]
    beyond = at_nodes(beyond, cols)
    ahead_ref[0:half, :] = jnp.where(even, beyond[0], last_lane(beyond[1]))
    ahead_ref[half : half + quarter, :] = jnp.where(
        even[:quarter], beyond[2][:quarter], last_lane(beyond[2][quarter:])
    )


def back_kernel(table, u_ref, load_ref, mod_ref, phase_ref, halo_ref, back_ref, work_ref):
    half, cols = u_ref.shape[2] // 2, u_ref.shape[3]
    summer, rows = Summer(table), Rows(work_ref)
    even_zero, odd_zero, top_zero = local_plane(rows, u_ref, halo_ref, 0)
    zero = plane_views(even_zero, odd_zero, top_zero)
    one = plane_views(*local_plane(rows, u_ref, halo_ref, 1))
    rows_zero = element_rows(rows, mod_ref, phase_ref, halo_ref, 0)
    even = even_lanes((half, cols))
    own = None
    for cy in range(2):
        elements = Elements(*rows_zero[cy])
        part = summer.force(
            elements, cy, terms_of(zero, 0, cy, 0, "o") + terms_of(one, 0, cy, 1, "so")
        )
        own = part if own is None else added(own, part)
        for k in range(2):
            back_ref[(6 + 2 * k + cy) * half : (7 + 2 * k + cy) * half, :] = rows_zero[cy][k]
    own = at_nodes(own, cols)
    back_ref[10 * half :, :] = jnp.zeros((8, cols), jnp.float32)
    for c in range(3):
        left = rows.split(load_ref[c, 0])[0] - own[c]
        back_ref[c * half : (c + 1) * half, :] = jnp.where(even, left, even_zero[c])
        back_ref[(3 + c) * half : (4 + c) * half, :] = odd_zero[c]
        back_ref[10 * half + c : 10 * half + c + 1, :] = top_zero[c]


def inner_kernel(table, u_ref, load_ref, mod_ref, phase_ref, halo_ref, sums_ref, work_ref):
    half, cols = u_ref.shape[2] // 2, u_ref.shape[3]
    summer, rows = Summer(table), Rows(work_ref)
    zero = plane_views(*local_plane(rows, u_ref, halo_ref, 0))
    one = plane_views(*local_plane(rows, u_ref, halo_ref, 1))
    rows_zero = element_rows(rows, mod_ref, phase_ref, halo_ref, 0)
    rows_one = element_rows(rows, mod_ref, phase_ref, halo_ref, 1)
    total, middle, first, last = None, None, None, None
    for cy in range(2):
        left, right = Elements(*rows_zero[cy]), Elements(*rows_one[cy])
        part = summer.force(left, 2 + cy, terms_of(zero, 1, cy, 0, "o") + terms_of(one, 1, cy, 1, "o"))
        part = added(part, summer.force(right, cy, terms_of(one, 0, cy, 0, "o")))
        total = part if total is None else added(total, part)
        near = summer.diagonal(left, cy)
        mid = added(summer.diagonal(left, 2 + cy), summer.diagonal(right, cy))
        far = summer.diagonal(right, 2 + cy)
        first = near if first is None else added(first, near)
        middle = mid if middle is None else added(middle, mid)
        last = far if last is None else added(last, far)
    total = at_nodes(total, cols)
    for c in range(3):
        sums_ref[c] = rows.split(load_ref[c, 1])[0] - total[c]
    solved = inverse_of(at_nodes(middle, cols))
    first = at_nodes(first, cols)
    last = at_nodes(last, cols)
    for k in range(9):
        sums_ref[3 + k] = solved[k]
        sums_ref[12 + k] = first[k]
        sums_ref[21 + k] = last[k]


def unpacked(a, half):
    quarter = half // 2
    block = a[0:half, :]
    rest = a[half : half + quarter, :]
    return [block, next_lane(block), jnp.concatenate([rest, next_lane(rest)], axis=0)]


def finish_kernel(
    table, u_ref, mod_ref, phase_ref, halo_ref, sums_ref, mine_back, mine_ahead, ahead_ref, odd_ref, top_ref, end_ref, out_ref, work_ref
):
    half, cols = u_ref.shape[2] // 2, u_ref.shape[3]
    quarter = half // 2
    back_ref = jnp.concatenate([top_ref[...], end_ref[...]], axis=0) + odd_ref[...]
    summer, rows = Summer(table), Rows(work_ref)
    even_zero, odd_zero, top_zero = local_plane(rows, u_ref, halo_ref, 0)
    zero = plane_views(even_zero, odd_zero, top_zero)
    rows_zero = element_rows(rows, mod_ref, phase_ref, halo_ref, 0)
    rows_one = element_rows(rows, mod_ref, phase_ref, halo_ref, 1)
    even_two = [back_ref[c * half : (c + 1) * half, :] for c in range(3)]
    odd_two = [back_ref[(3 + c) * half : (4 + c) * half, :] for c in range(3)]
    top_two = [back_ref[10 * half + c : 10 * half + c + 1, :] for c in range(3)]
    two = plane_views(even_two, odd_two, top_two)
    even = even_lanes((half, cols))
    before, after, lower, upper, beyond = None, None, None, None, None
    for cy in range(2):
        start = half + quarter + cy * half
        minus = Elements(ahead_ref[start : start + half, :], ahead_ref[start + 2 * half : start + 3 * half, :])
        start = (6 + cy) * half
        plus = Elements(back_ref[start : start + half, :], back_ref[start + 2 * half : start + 3 * half, :])
        right = Elements(*rows_one[cy])
        part = summer.force(minus, 2 + cy, terms_of(zero, 1, cy, 1, "o"))
        before = part if before is None else added(before, part)
        part = summer.force(right, 2 + cy, terms_of(two, 1, cy, 1, "o"))
        after = part if after is None else added(after, part)
        part = summer.force(right, cy, terms_of(two, 0, cy, 1, "o"))
        beyond = part if beyond is None else added(beyond, part)
        part = summer.diagonal(minus, 2 + cy)
        lower = part if lower is None else added(lower, part)
        part = summer.diagonal(plus, cy)
        upper = part if upper is None else added(upper, part)
    before, after = at_nodes(before, cols), at_nodes(after, cols)
    lower, upper = at_nodes(lower, cols), at_nodes(upper, cols)
    came, sent = unpacked(ahead_ref, half), unpacked(mine_ahead, half)
    right = [mine_back[c * half : (c + 1) * half, :] - came[c] - before[c] for c in range(3)]
    first_new = applied(inverse_of([sums_ref[12 + k] + lower[k] for k in range(9)]), right)
    right = [even_two[c] - sent[c] - after[c] for c in range(3)]
    third_new = applied(inverse_of([sums_ref[21 + k] + upper[k] for k in range(9)]), right)
    near = [pair_even(a)["s"] for a in first_new]
    far = [pair_even(a)["s"] for a in third_new]
    for cy in range(2):
        left, right = Elements(*rows_zero[cy]), Elements(*rows_one[cy])
        beyond = added(beyond, summer.force(left, 2 + cy, [(cy, "s", near)]))
        beyond = added(beyond, summer.force(right, cy, [(2 + cy, "s", far)]))
    beyond = at_nodes(beyond, cols)
    solved = [sums_ref[3 + k] for k in range(9)]
    second_new = applied(solved, [sums_ref[c] - beyond[c] for c in range(3)])
    for c in range(3):
        out_ref[c, 0] = rows.merge(jnp.where(even, first_new[c], even_zero[c]), odd_zero[c])
        own, other = rows.split(u_ref[c, 1])
        out_ref[c, 1] = rows.merge(jnp.where(even, second_new[c], own), other)


def whole():
    return pl.BlockSpec(memory_space=pltpu.VMEM)


def scalars():
    return pl.BlockSpec(memory_space=pltpu.SMEM)


def on_device(displacement, load, element_phase, element_modulus, stiffness):
    planes, rows, cols = displacement.shape[1:]
    half = rows // 2
    kind = displacement.dtype
    table = stiffness.reshape(-1)
    last = rows // 8 - 1
    slots = 16
    rim = pl.pallas_call(
        rim_kernel,
        grid=(1,),
        in_specs=[
            pl.BlockSpec((3, planes, 8, cols), lambda i: (0, 0, last, 0)),
            pl.BlockSpec((planes, 8, cols), lambda i: (0, last, 0)),
            pl.BlockSpec((planes, 8, cols), lambda i: (0, last, 0)),
        ],
        out_specs=pl.BlockSpec((16, cols), lambda i: (0, 0)),
        out_shape=jax.ShapeDtypeStruct((16, cols), kind),
    )(displacement, element_modulus, element_phase)
    halo = shifted(rim, "gy", 1)
    back_rows, ahead_rows = 10 * half + 8, 5 * half + half // 2
    params = pltpu.CompilerParams(vmem_limit_bytes=24 << 20)
    scratch = [pltpu.VMEM((slots, cols // 128, rows, 128), kind)]
    ahead_shape = jax.ShapeDtypeStruct((ahead_rows, cols), kind)
    back_shape = jax.ShapeDtypeStruct((back_rows, cols), kind)
    part_shape = jax.ShapeDtypeStruct((back_rows // 2, cols), kind)
    back = pl.pallas_call(
        back_kernel,
        in_specs=[scalars()] + [whole()] * 5,
        out_specs=whole(),
        out_shape=back_shape,
        scratch_shapes=scratch,
        compiler_params=params,
    )(table, displacement, load, element_modulus, element_phase, halo)
    from_odd = shifted_from(back, "gx", -1, 1)
    ahead, top, end = pl.pallas_call(
        ahead_kernel,
        in_specs=[scalars()] + [whole()] * 5,
        out_specs=[whole()] * 3,
        out_shape=[ahead_shape, part_shape, part_shape],
        scratch_shapes=scratch,
        compiler_params=params,
    )(table, displacement, element_modulus, element_phase, halo, back)
    from_last = shifted(ahead, "gx", 1)
    from_even = [shifted_from(part, "gx", -1, 0) for part in (top, end)]
    sums = pl.pallas_call(
        inner_kernel,
        in_specs=[scalars()] + [whole()] * 5,
        out_specs=whole(),
        out_shape=jax.ShapeDtypeStruct((30, half, cols), kind),
        scratch_shapes=scratch,
        compiler_params=params,
        cost_estimate=pl.CostEstimate(flops=20_000_000, bytes_accessed=1_000_000, transcendentals=0),
    )(table, displacement, load, element_modulus, element_phase, halo)
    return pl.pallas_call(
        finish_kernel,
        in_specs=[scalars()] + [whole()] * 11,
        out_specs=whole(),
        out_shape=jax.ShapeDtypeStruct(displacement.shape, kind),
        scratch_shapes=scratch,
        compiler_params=params,
    )(
        table, displacement, element_modulus, element_phase, halo, sums, back, ahead, from_last, from_odd, *from_even
    )


def solution(mesh):
    in_specs = (
        P(None, "gx", "gy", None),
        P(None, "gx", "gy", None),
        P("gx", "gy", None),
        P("gx", "gy", None),
        P(),
    )
    out_specs = P(None, "gx", "gy", None)
    return jax.shard_map(
        on_device, mesh=mesh, in_specs=in_specs, out_specs=out_specs, check_vma=False
    )
```

```python
import jax
import jax.numpy as jnp
from jax import lax
from jax.experimental import pallas as pl
from jax.experimental.pallas import tpu as pltpu
from jax.sharding import PartitionSpec as P

PARITY = {"0": (0, 0), "1": (1, 1), "s": (0, 1), "o": (1, 0)}


def shifted(x, axis, by):
    devices = lax.axis_size(axis)
    return lax.ppermute(x, axis, [(i, (i + by) % devices) for i in range(devices)])


def shifted_from(x, axis, by, parity):
    devices = lax.axis_size(axis)
    return lax.ppermute(x, axis, [(i, (i + by) % devices) for i in range(parity, devices, 2)])


def tiles(a):
    rows, cols = a.shape
    return jnp.stack(
        [a[r : r + 8, c : c + 128] for r in range(0, rows, 8) for c in range(0, cols, 128)]
    )


def flat(t, cols):
    across = cols // 128
    rows = [
        jnp.concatenate([t[r + c] for c in range(across)], axis=1)
        for r in range(0, t.shape[0], across)
    ]
    return jnp.concatenate(rows, axis=0)


def even_lanes(shape):
    return lax.broadcasted_iota(jnp.int32, shape, len(shape) - 1) % 2 == 0


def next_lane(a):
    return pltpu.roll(a, a.shape[-1] - 1, a.ndim - 1)


def last_lane(a):
    return pltpu.roll(a, 1, a.ndim - 1)


def down_row(a, top):
    first = lax.broadcasted_iota(jnp.int32, a.shape, 0) == 0
    return jnp.where(first, jnp.broadcast_to(top, a.shape), pltpu.roll(a, 1, 0))


def pair_even(a):
    here, there = tiles(a), tiles(next_lane(a))
    even = even_lanes((8, 128))[None]
    return {"s": jnp.where(even, here, there), "o": jnp.where(even, there, here)}


def pair_odd(a):
    return {"0": tiles(a), "1": tiles(next_lane(a))}


def plane_views(even_rows, odd_rows, tops):
    same = [pair_even(a) for a in even_rows]
    after = [pair_odd(a) for a in odd_rows]
    before = [pair_odd(down_row(a, top)) for a, top in zip(odd_rows, tops)]
    return same, after, before


class Elements:
    def __init__(self, modulus, phase):
        phase = tiles(phase)
        self.modulus, self.first, self.second = tiles(modulus), phase == 0, phase == 1


def coefficient(corner, partner, kind, i, j):
    return ((corner * 4 + partner) * 2 + ("0s1o".index(kind) // 2)) * 9 + i * 3 + j


PHASE_ROWS = 4 * 4 * 2 * 9


def fill_coefficients(table, tiles_ref):
    even = even_lanes((8, 128))
    for ph in range(3):
        for corner in range(4):
            for partner in range(4):
                for kind in "so" if partner % 2 == corner % 2 else "01":
                    for i in range(3):
                        for j in range(3):
                            places = [
                                table[(((ph * 8 + corner * 2 + parity) * 8 + partner * 2 + side) * 3 + i) * 3 + j]
                                for parity, side in enumerate(PARITY[kind])
                            ]
                            row = ph * PHASE_ROWS + coefficient(corner, partner, kind, i, j)
                            tiles_ref[row] = jnp.where(even, places[0], places[1])


class Summer:
    def __init__(self, tiles_ref):
        self.tiles = tiles_ref

    def entry(self, elements, corner, partner, kind, i, j):
        row = coefficient(corner, partner, kind, i, j)
        picked = [self.tiles[ph * PHASE_ROWS + row][None] for ph in range(3)]
        return jnp.where(elements.first, picked[0], jnp.where(elements.second, picked[1], picked[2]))

    def force(self, elements, corner, terms):
        total = [None] * 3
        for partner, kind, values in terms:
            for i in range(3):
                for j in range(3):
                    part = self.entry(elements, corner, partner, kind, i, j) * values[j]
                    total[i] = part if total[i] is None else total[i] + part
        return [elements.modulus * part for part in total]

    def diagonal(self, elements, corner):
        return [
            elements.modulus * self.entry(elements, corner, corner, "s", i, j)
            for i in range(3)
            for j in range(3)
        ]


def pick(views, kind):
    return [view[kind] for view in views]


def terms_of(views, cx, cy, dx, kinds):
    same, after, before = views
    other = after if cy == 0 else before
    found = [(dx * 2 + cy, kind, pick(same, kind)) for kind in kinds]
    found += [(dx * 2 + 1 - cy, kind, pick(other, kind)) for kind in ("0", "1")]
    return found


def added(left, right):
    return [a + b for a, b in zip(left, right)]


def at_nodes(parts, cols):
    out = []
    for part in parts:
        whole = flat(part, cols)
        out.append(whole + last_lane(whole))
    return out


def inverse_of(m):
    m00, m01, m02, m10, m11, m12, m20, m21, m22 = m
    c00 = m11 * m22 - m12 * m21
    c01 = m12 * m20 - m10 * m22
    c02 = m10 * m21 - m11 * m20
    c10 = m02 * m21 - m01 * m22
    c11 = m00 * m22 - m02 * m20
    c12 = m01 * m20 - m00 * m21
    c20 = m01 * m12 - m02 * m11
    c21 = m02 * m10 - m00 * m12
    c22 = m00 * m11 - m01 * m10
    determinant = m00 * c00 + m01 * c01 + m02 * c02
    scale = 1.0 / determinant
    return [a * scale for a in (c00, c10, c20, c01, c11, c21, c02, c12, c22)]


def applied(inverse, right):
    return [sum(inverse[3 * i + j] * right[j] for j in range(3)) for i in range(3)]


class Rows:
    def __init__(self, work_ref):
        self.work, self.slot = work_ref, 0

    def split(self, a):
        parts, slot, half = a.shape[1] // 128, self.slot, a.shape[0] // 2
        self.slot += 1
        for k in range(parts):
            self.work[slot, k] = a[:, k * 128 : (k + 1) * 128]
        return tuple(
            jnp.concatenate([self.work[slot, k, pl.ds(bit, half, 2), :] for k in range(parts)], axis=1)
            for bit in range(2)
        )

    def merge(self, even, odd):
        parts, slot, half = even.shape[1] // 128, self.slot, even.shape[0]
        self.slot += 1
        for k in range(parts):
            self.work[slot, k, pl.ds(0, half, 2), :] = even[:, k * 128 : (k + 1) * 128]
            self.work[slot, k, pl.ds(1, half, 2), :] = odd[:, k * 128 : (k + 1) * 128]
        return jnp.concatenate([self.work[slot, k] for k in range(parts)], axis=1)


def halo_row(halo_ref, row, cols):
    return jnp.zeros((1, cols), jnp.float32) if halo_ref is None else halo_ref[row : row + 1, :]


def local_plane(rows, u_ref, halo_ref, plane):
    split = [rows.split(u_ref[c, plane]) for c in range(3)]
    even, odd = [a for a, _ in split], [b for _, b in split]
    tops = [halo_row(halo_ref, 3 * plane + c, u_ref.shape[-1]) for c in range(3)]
    return even, odd, tops


def element_rows(rows, mod_ref, phase_ref, halo_ref, plane):
    split = [rows.split(mod_ref[plane]), rows.split(phase_ref[plane].astype(jnp.float32))]
    even, odd = [a for a, _ in split], [b for _, b in split]
    before = (
        down_row(odd[0], halo_row(halo_ref, 6 + plane, mod_ref.shape[-1])),
        down_row(odd[1], halo_row(halo_ref, 8 + plane, mod_ref.shape[-1])),
    )
    return even, before


def fetch_kernel(u_hbm, load_hbm, mod_hbm, phase_hbm, out_ref, u_ref, load_ref, mod_ref, phase_ref, sems):
    copies = [
        pltpu.make_async_copy(source, target, sems.at[k])
        for k, (source, target) in enumerate(
            ((u_hbm, u_ref), (mod_hbm, mod_ref), (phase_hbm, phase_ref), (load_hbm, load_ref))
        )
    ]
    for copy in copies:
        copy.start()
    for copy in copies[:3]:
        copy.wait()
    last = u_ref.shape[2] - 1
    for plane in range(2):
        for c in range(3):
            out_ref[3 * plane + c : 3 * plane + c + 1, :] = u_ref[c, plane, last : last + 1, :]
        out_ref[6 + plane : 7 + plane, :] = mod_ref[plane, last : last + 1, :]
        out_ref[8 + plane : 9 + plane, :] = phase_ref[plane, last : last + 1, :].astype(jnp.float32)
    out_ref[10:16, :] = jnp.zeros((6, out_ref.shape[1]), jnp.float32)
    copies[3].wait()


def prepare_kernel(table, u_ref, load_ref, mod_ref, phase_ref, tiles_ref, back_ref, ahead_ref, work_ref):
    half, cols = u_ref.shape[2] // 2, u_ref.shape[3]
    quarter = half // 2
    fill_coefficients(table, tiles_ref)
    summer, rows = Summer(tiles_ref), Rows(work_ref)
    even_zero, odd_zero, top_zero = local_plane(rows, u_ref, None, 0)
    zero = plane_views(even_zero, odd_zero, top_zero)
    one = plane_views(*local_plane(rows, u_ref, None, 1))
    rows_zero = element_rows(rows, mod_ref, phase_ref, None, 0)
    rows_one = element_rows(rows, mod_ref, phase_ref, None, 1)
    even = even_lanes((half, cols))
    own, beyond = None, None
    for cy in range(2):
        elements = Elements(*rows_zero[cy])
        part = summer.force(
            elements, cy, terms_of(zero, 0, cy, 0, "o") + terms_of(one, 0, cy, 1, "so")
        )
        own = part if own is None else added(own, part)
        elements = Elements(*rows_one[cy])
        part = summer.force(elements, 2 + cy, terms_of(one, 1, cy, 0, "so"))
        beyond = part if beyond is None else added(beyond, part)
        for k in range(2):
            start = (6 + 2 * k + cy) * half
            back_ref[start : start + half, :] = rows_zero[cy][k]
            start = half + quarter + (2 * k + cy) * half
            ahead_ref[start : start + half, :] = rows_one[cy][k]
    own, beyond = at_nodes(own, cols), at_nodes(beyond, cols)
    back_ref[10 * half :, :] = jnp.zeros((8, cols), jnp.float32)
    for c in range(3):
        left = rows.split(load_ref[c, 0])[0] - own[c]
        back_ref[c * half : (c + 1) * half, :] = jnp.where(even, left, even_zero[c])
        back_ref[(3 + c) * half : (4 + c) * half, :] = odd_zero[c]
    ahead_ref[0:half, :] = jnp.where(even, beyond[0], last_lane(beyond[1]))
    ahead_ref[half : half + quarter, :] = jnp.where(
        even[:quarter], beyond[2][:quarter], last_lane(beyond[2][quarter:])
    )


def top_kernel(
    tiles_ref, u_ref, halo_ref, back_in, ahead_in, back_ref, ahead_ref, first_ref, second_ref
):
    half, cols = u_ref.shape[2] // 2, u_ref.shape[3]
    quarter = half // 2
    summer = Summer(tiles_ref)

    def wide(row):
        return jnp.broadcast_to(row, (8, cols))

    views, corners = [], []
    for plane in range(2):
        before = [wide(halo_ref[3 * plane + c : 3 * plane + c + 1, :]) for c in range(3)]
        same = [wide(u_ref[c, plane, 0:1, :]) for c in range(3)]
        views.append(([pair_even(a) for a in same], None, [pair_odd(a) for a in before]))
        corners.append(
            Elements(wide(halo_ref[6 + plane : 7 + plane, :]), wide(halo_ref[8 + plane : 9 + plane, :]))
        )
    own = summer.force(
        corners[0], 1, terms_of(views[0], 0, 1, 0, "o") + terms_of(views[1], 0, 1, 1, "so")
    )
    beyond = summer.force(corners[1], 3, terms_of(views[1], 1, 1, 0, "so"))
    own, beyond = at_nodes(own, cols), at_nodes(beyond, cols)
    even = even_lanes((1, cols))
    back_ref[...] = back_in[...]
    ahead_ref[...] = ahead_in[...]
    for c in range(3):
        old = back_in[c * half : c * half + 1, :]
        back_ref[c * half : c * half + 1, :] = jnp.where(even, old - own[c][0:1], old)
    back_ref[10 * half : 10 * half + 3, :] = halo_ref[0:3, :]
    for k in range(2):
        start = (7 + 2 * k) * half
        back_ref[start : start + 1, :] = halo_ref[6 + 2 * k : 7 + 2 * k, :]
        start = half + quarter + (2 * k + 1) * half
        ahead_ref[start : start + 1, :] = halo_ref[7 + 2 * k : 8 + 2 * k, :]
    ahead_ref[0:1, :] = ahead_in[0:1, :] + jnp.where(even, beyond[0][0:1], last_lane(beyond[1])[0:1])
    ahead_ref[half : half + 1, :] = jnp.where(
        even, ahead_in[half : half + 1, :] + beyond[2][0:1], ahead_in[half : half + 1, :]
    )
    first_ref[...] = back_ref[: first_ref.shape[0], :]
    second_ref[...] = back_ref[first_ref.shape[0] :, :]


def inner_kernel(tiles_ref, u_ref, load_ref, mod_ref, phase_ref, halo_ref, sums_ref, work_ref):
    half, cols = u_ref.shape[2] // 2, u_ref.shape[3]
    summer, rows = Summer(tiles_ref), Rows(work_ref)
    zero = plane_views(*local_plane(rows, u_ref, halo_ref, 0))
    one = plane_views(*local_plane(rows, u_ref, halo_ref, 1))
    rows_zero = element_rows(rows, mod_ref, phase_ref, halo_ref, 0)
    rows_one = element_rows(rows, mod_ref, phase_ref, halo_ref, 1)
    total, middle, first, last = None, None, None, None
    for cy in range(2):
        left, right = Elements(*rows_zero[cy]), Elements(*rows_one[cy])
        part = summer.force(left, 2 + cy, terms_of(zero, 1, cy, 0, "o") + terms_of(one, 1, cy, 1, "o"))
        part = added(part, summer.force(right, cy, terms_of(one, 0, cy, 0, "o")))
        total = part if total is None else added(total, part)
        near = summer.diagonal(left, cy)
        mid = added(summer.diagonal(left, 2 + cy), summer.diagonal(right, cy))
        far = summer.diagonal(right, 2 + cy)
        first = near if first is None else added(first, near)
        middle = mid if middle is None else added(middle, mid)
        last = far if last is None else added(last, far)
    total = at_nodes(total, cols)
    for c in range(3):
        sums_ref[c] = rows.split(load_ref[c, 1])[0] - total[c]
    solved = inverse_of(at_nodes(middle, cols))
    first = at_nodes(first, cols)
    last = at_nodes(last, cols)
    for k in range(9):
        sums_ref[3 + k] = solved[k]
        sums_ref[12 + k] = first[k]
        sums_ref[21 + k] = last[k]


def unpacked(a, half):
    quarter = half // 2
    block = a[0:half, :]
    rest = a[half : half + quarter, :]
    return [block, next_lane(block), jnp.concatenate([rest, next_lane(rest)], axis=0)]


def finish_kernel(
    tiles_ref, u_ref, mod_ref, phase_ref, halo_ref, sums_ref, mine_back, mine_ahead, ahead_ref, odd_ref, top_ref, end_ref, out_ref, work_ref
):
    half, cols = u_ref.shape[2] // 2, u_ref.shape[3]
    quarter = half // 2
    back_ref = jnp.concatenate([top_ref[...], end_ref[...]], axis=0) + odd_ref[...]
    summer, rows = Summer(tiles_ref), Rows(work_ref)
    even_zero, odd_zero, top_zero = local_plane(rows, u_ref, halo_ref, 0)
    zero = plane_views(even_zero, odd_zero, top_zero)
    rows_zero = element_rows(rows, mod_ref, phase_ref, halo_ref, 0)
    rows_one = element_rows(rows, mod_ref, phase_ref, halo_ref, 1)
    even_two = [back_ref[c * half : (c + 1) * half, :] for c in range(3)]
    odd_two = [back_ref[(3 + c) * half : (4 + c) * half, :] for c in range(3)]
    top_two = [back_ref[10 * half + c : 10 * half + c + 1, :] for c in range(3)]
    two = plane_views(even_two, odd_two, top_two)
    even = even_lanes((half, cols))
    before, after, lower, upper, beyond = None, None, None, None, None
    for cy in range(2):
        start = half + quarter + cy * half
        minus = Elements(ahead_ref[start : start + half, :], ahead_ref[start + 2 * half : start + 3 * half, :])
        start = (6 + cy) * half
        plus = Elements(back_ref[start : start + half, :], back_ref[start + 2 * half : start + 3 * half, :])
        right = Elements(*rows_one[cy])
        part = summer.force(minus, 2 + cy, terms_of(zero, 1, cy, 1, "o"))
        before = part if before is None else added(before, part)
        part = summer.force(right, 2 + cy, terms_of(two, 1, cy, 1, "o"))
        after = part if after is None else added(after, part)
        part = summer.force(right, cy, terms_of(two, 0, cy, 1, "o"))
        beyond = part if beyond is None else added(beyond, part)
        part = summer.diagonal(minus, 2 + cy)
        lower = part if lower is None else added(lower, part)
        part = summer.diagonal(plus, cy)
        upper = part if upper is None else added(upper, part)
    before, after = at_nodes(before, cols), at_nodes(after, cols)
    lower, upper = at_nodes(lower, cols), at_nodes(upper, cols)
    came, sent = unpacked(ahead_ref, half), unpacked(mine_ahead, half)
    right = [mine_back[c * half : (c + 1) * half, :] - came[c] - before[c] for c in range(3)]
    first_new = applied(inverse_of([sums_ref[12 + k] + lower[k] for k in range(9)]), right)
    right = [even_two[c] - sent[c] - after[c] for c in range(3)]
    third_new = applied(inverse_of([sums_ref[21 + k] + upper[k] for k in range(9)]), right)
    near = [pair_even(a)["s"] for a in first_new]
    far = [pair_even(a)["s"] for a in third_new]
    for cy in range(2):
        left, right = Elements(*rows_zero[cy]), Elements(*rows_one[cy])
        beyond = added(beyond, summer.force(left, 2 + cy, [(cy, "s", near)]))
        beyond = added(beyond, summer.force(right, cy, [(2 + cy, "s", far)]))
    beyond = at_nodes(beyond, cols)
    solved = [sums_ref[3 + k] for k in range(9)]
    second_new = applied(solved, [sums_ref[c] - beyond[c] for c in range(3)])
    for c in range(3):
        out_ref[c, 0] = rows.merge(jnp.where(even, first_new[c], even_zero[c]), odd_zero[c])
        own, other = rows.split(u_ref[c, 1])
        out_ref[c, 1] = rows.merge(jnp.where(even, second_new[c], own), other)


def whole():
    return pl.BlockSpec(memory_space=pltpu.VMEM)


def scalars():
    return pl.BlockSpec(memory_space=pltpu.SMEM)


def on_device(displacement, load, element_phase, element_modulus, stiffness):
    planes, rows, cols = displacement.shape[1:]
    half = rows // 2
    kind = displacement.dtype
    table = stiffness.reshape(-1)
    slots = 16
    rim, displacement, load, element_modulus, element_phase = pl.pallas_call(
        fetch_kernel,
        in_specs=[pl.BlockSpec(memory_space=pl.ANY)] * 4,
        out_specs=[whole()] * 5,
        out_shape=[jax.ShapeDtypeStruct((16, cols), kind)]
        + [jax.ShapeDtypeStruct(a.shape, a.dtype) for a in (displacement, load, element_modulus, element_phase)],
        scratch_shapes=[pltpu.SemaphoreType.DMA((4,))],
        compiler_params=pltpu.CompilerParams(vmem_limit_bytes=8 << 20),
        cost_estimate=pl.CostEstimate(flops=1_000_000_000, bytes_accessed=0, transcendentals=0),
    )(*(pltpu.with_memory_space_constraint(a, pltpu.HBM) for a in (displacement, load, element_modulus, element_phase)))
    halo = shifted(rim, "gy", 1)
    back_rows, ahead_rows = 10 * half + 8, 5 * half + half // 2
    params = pltpu.CompilerParams(vmem_limit_bytes=24 << 20)
    scratch = [pltpu.VMEM((slots, cols // 128, rows, 128), kind)]
    ahead_shape = jax.ShapeDtypeStruct((ahead_rows, cols), kind)
    back_shape = jax.ShapeDtypeStruct((back_rows, cols), kind)
    part_shape = jax.ShapeDtypeStruct((back_rows // 2, cols), kind)
    tile_shape = jax.ShapeDtypeStruct((3 * PHASE_ROWS, 8, 128), kind)
    coefficients, back, ahead = pl.pallas_call(
        prepare_kernel,
        in_specs=[scalars()] + [whole()] * 4,
        out_specs=[whole()] * 3,
        out_shape=[tile_shape, back_shape, ahead_shape],
        scratch_shapes=scratch,
        compiler_params=params,
        cost_estimate=pl.CostEstimate(flops=20_000_000, bytes_accessed=6_000_000, transcendentals=0),
    )(table, displacement, load, element_modulus, element_phase)
    back, ahead, top, end = pl.pallas_call(
        top_kernel,
        in_specs=[whole()] * 5,
        out_specs=[whole()] * 4,
        out_shape=[back_shape, ahead_shape, part_shape, part_shape],
        compiler_params=params,
    )(coefficients, displacement, halo, back, ahead)
    from_odd = shifted_from(back, "gx", -1, 1)
    from_last = shifted(ahead, "gx", 1)
    from_even = [shifted_from(part, "gx", -1, 0) for part in (top, end)]
    sums = pl.pallas_call(
        inner_kernel,
        in_specs=[whole()] * 6,
        out_specs=whole(),
        out_shape=jax.ShapeDtypeStruct((30, half, cols), kind),
        scratch_shapes=scratch,
        compiler_params=params,
        cost_estimate=pl.CostEstimate(flops=20_000_000, bytes_accessed=1_000_000, transcendentals=0),
    )(coefficients, displacement, load, element_modulus, element_phase, halo)
    return pl.pallas_call(
        finish_kernel,
        in_specs=[whole()] * 12,
        out_specs=whole(),
        out_shape=jax.ShapeDtypeStruct(displacement.shape, kind),
        scratch_shapes=scratch,
        compiler_params=params,
    )(
        coefficients, displacement, element_modulus, element_phase, halo, sums, back, ahead, from_last, from_odd, *from_even
    )


def solution(mesh):
    in_specs = (
        P(None, "gx", "gy", None),
        P(None, "gx", "gy", None),
        P("gx", "gy", None),
        P("gx", "gy", None),
        P(),
    )
    out_specs = P(None, "gx", "gy", None)
    return jax.shard_map(
        on_device, mesh=mesh, in_specs=in_specs, out_specs=out_specs, check_vma=False
    )
```

```python
import jax
import jax.numpy as jnp
from jax import lax
from jax.experimental import pallas as pl
from jax.experimental.pallas import tpu as pltpu
from jax.sharding import PartitionSpec as P

PARITY = {"0": (0, 0), "1": (1, 1), "s": (0, 1), "o": (1, 0)}


def shifted(x, axis, by):
    devices = lax.axis_size(axis)
    return lax.ppermute(x, axis, [(i, (i + by) % devices) for i in range(devices)])


def shifted_from(x, axis, by, parity):
    devices = lax.axis_size(axis)
    return lax.ppermute(x, axis, [(i, (i + by) % devices) for i in range(parity, devices, 2)])


def tiles(a):
    rows, cols = a.shape
    return jnp.stack(
        [a[r : r + 8, c : c + 128] for r in range(0, rows, 8) for c in range(0, cols, 128)]
    )


def flat(t, cols):
    across = cols // 128
    rows = [
        jnp.concatenate([t[r + c] for c in range(across)], axis=1)
        for r in range(0, t.shape[0], across)
    ]
    return jnp.concatenate(rows, axis=0)


def even_lanes(shape):
    return lax.broadcasted_iota(jnp.int32, shape, len(shape) - 1) % 2 == 0


def next_lane(a):
    return pltpu.roll(a, a.shape[-1] - 1, a.ndim - 1)


def last_lane(a):
    return pltpu.roll(a, 1, a.ndim - 1)


def down_row(a, top):
    first = lax.broadcasted_iota(jnp.int32, a.shape, 0) == 0
    return jnp.where(first, jnp.broadcast_to(top, a.shape), pltpu.roll(a, 1, 0))


def pair_even(a):
    here, there = tiles(a), tiles(next_lane(a))
    even = even_lanes((8, 128))[None]
    return {"s": jnp.where(even, here, there), "o": jnp.where(even, there, here)}


def pair_odd(a):
    return {"0": tiles(a), "1": tiles(next_lane(a))}


def plane_views(even_rows, odd_rows, tops):
    same = [pair_even(a) for a in even_rows]
    after = [pair_odd(a) for a in odd_rows]
    before = [pair_odd(down_row(a, top)) for a, top in zip(odd_rows, tops)]
    return same, after, before


class Elements:
    def __init__(self, modulus, phase):
        phase = tiles(phase)
        self.modulus, self.first, self.second = tiles(modulus), phase == 0, phase == 1


def coefficient(corner, partner, kind, i, j):
    return ((corner * 4 + partner) * 2 + ("0s1o".index(kind) // 2)) * 9 + i * 3 + j


PHASE_ROWS = 4 * 4 * 2 * 9


def fill_coefficients(table, tiles_ref):
    even = even_lanes((8, 128))
    for ph in range(3):
        for corner in range(4):
            for partner in range(4):
                for kind in "so" if partner % 2 == corner % 2 else "01":
                    for i in range(3):
                        for j in range(3):
                            places = [
                                table[(((ph * 8 + corner * 2 + parity) * 8 + partner * 2 + side) * 3 + i) * 3 + j]
                                for parity, side in enumerate(PARITY[kind])
                            ]
                            row = ph * PHASE_ROWS + coefficient(corner, partner, kind, i, j)
                            tiles_ref[row] = jnp.where(even, places[0], places[1])


class Summer:
    def __init__(self, tiles_ref):
        self.tiles = tiles_ref

    def entry(self, elements, corner, partner, kind, i, j):
        row = coefficient(corner, partner, kind, i, j)
        picked = [self.tiles[ph * PHASE_ROWS + row][None] for ph in range(3)]
        return jnp.where(elements.first, picked[0], jnp.where(elements.second, picked[1], picked[2]))

    def force(self, elements, corner, terms):
        total = [None] * 3
        for partner, kind, values in terms:
            for i in range(3):
                for j in range(3):
                    part = self.entry(elements, corner, partner, kind, i, j) * values[j]
                    total[i] = part if total[i] is None else total[i] + part
        return [elements.modulus * part for part in total]

    def diagonal(self, elements, corner):
        return [
            elements.modulus * self.entry(elements, corner, corner, "s", i, j)
            for i in range(3)
            for j in range(3)
        ]


def pick(views, kind):
    return [view[kind] for view in views]


def terms_of(views, cx, cy, dx, kinds):
    same, after, before = views
    other = after if cy == 0 else before
    found = [(dx * 2 + cy, kind, pick(same, kind)) for kind in kinds]
    found += [(dx * 2 + 1 - cy, kind, pick(other, kind)) for kind in ("0", "1")]
    return found


OWN_TERMS = [
    (cx, corner, partner, kind)
    for cy in range(2)
    for cx, corner, partners in ((0, 2 + cy, ((cy, "s"),)), (1, cy, None), (1, 2 + cy, None))
    for partner, kind in (
        partners
        or (
            ([(2 + cy, "s")] if corner < 2 else [])
            + [(2 + cy, "o"), (3 - cy, "0"), (3 - cy, "1")]
        )
    )
]


def weigh_own(summer, elements, own_ref):
    for place, (plane, corner, partner, kind) in enumerate(OWN_TERMS):
        part = elements[plane][corner % 2]
        for i in range(3):
            for j in range(3):
                own_ref[place * 9 + i * 3 + j] = part.modulus * summer.entry(part, corner, partner, kind, i, j)


def own_force(own_ref, plane, corner, terms):
    total = [None] * 3
    for partner, kind, values in terms:
        place = OWN_TERMS.index((plane, corner, partner, kind))
        for i in range(3):
            for j in range(3):
                part = own_ref[place * 9 + i * 3 + j] * values[j]
                total[i] = part if total[i] is None else total[i] + part
    return total


def added(left, right):
    return [a + b for a, b in zip(left, right)]


def at_nodes(parts, cols):
    out = []
    for part in parts:
        whole = flat(part, cols)
        out.append(whole + last_lane(whole))
    return out


def inverse_of(m):
    m00, m01, m02, m10, m11, m12, m20, m21, m22 = m
    c00 = m11 * m22 - m12 * m21
    c01 = m12 * m20 - m10 * m22
    c02 = m10 * m21 - m11 * m20
    c10 = m02 * m21 - m01 * m22
    c11 = m00 * m22 - m02 * m20
    c12 = m01 * m20 - m00 * m21
    c20 = m01 * m12 - m02 * m11
    c21 = m02 * m10 - m00 * m12
    c22 = m00 * m11 - m01 * m10
    determinant = m00 * c00 + m01 * c01 + m02 * c02
    scale = 1.0 / determinant
    return [a * scale for a in (c00, c10, c20, c01, c11, c21, c02, c12, c22)]


def applied(inverse, right):
    return [sum(inverse[3 * i + j] * right[j] for j in range(3)) for i in range(3)]


class Rows:
    def __init__(self, work_ref):
        self.work, self.slot = work_ref, 0

    def split(self, a):
        parts, slot, half = a.shape[1] // 128, self.slot, a.shape[0] // 2
        self.slot += 1
        for k in range(parts):
            self.work[slot, k] = a[:, k * 128 : (k + 1) * 128]
        return tuple(
            jnp.concatenate([self.work[slot, k, pl.ds(bit, half, 2), :] for k in range(parts)], axis=1)
            for bit in range(2)
        )

    def merge(self, even, odd):
        parts, slot, half = even.shape[1] // 128, self.slot, even.shape[0]
        self.slot += 1
        for k in range(parts):
            self.work[slot, k, pl.ds(0, half, 2), :] = even[:, k * 128 : (k + 1) * 128]
            self.work[slot, k, pl.ds(1, half, 2), :] = odd[:, k * 128 : (k + 1) * 128]
        return jnp.concatenate([self.work[slot, k] for k in range(parts)], axis=1)


def halo_row(halo_ref, row, cols):
    return jnp.zeros((1, cols), jnp.float32) if halo_ref is None else halo_ref[row : row + 1, :]


def local_plane(rows, u_ref, halo_ref, plane):
    split = [rows.split(u_ref[c, plane]) for c in range(3)]
    even, odd = [a for a, _ in split], [b for _, b in split]
    tops = [halo_row(halo_ref, 3 * plane + c, u_ref.shape[-1]) for c in range(3)]
    return even, odd, tops


def element_rows(rows, mod_ref, phase_ref, halo_ref, plane):
    split = [rows.split(mod_ref[plane]), rows.split(phase_ref[plane].astype(jnp.float32))]
    even, odd = [a for a, _ in split], [b for _, b in split]
    before = (
        down_row(odd[0], halo_row(halo_ref, 6 + plane, mod_ref.shape[-1])),
        down_row(odd[1], halo_row(halo_ref, 8 + plane, mod_ref.shape[-1])),
    )
    return even, before


def started(sources, targets, sems):
    copies = [
        pltpu.make_async_copy(source, target, sems.at[k])
        for k, (source, target) in enumerate(zip(sources, targets))
    ]
    for copy in copies:
        copy.start()
    return copies


def rim_kernel(u_hbm, mod_hbm, phase_hbm, out_ref, u_ref, mod_ref, phase_ref, sems):
    edge = pl.ds(u_hbm.shape[2] - 8, 8)
    sources = (u_hbm.at[:, :, edge, :], mod_hbm.at[:, edge, :], phase_hbm.at[:, edge, :])
    for copy in started(sources, (u_ref, mod_ref, phase_ref), sems):
        copy.wait()
    for plane in range(2):
        for c in range(3):
            out_ref[3 * plane + c : 3 * plane + c + 1, :] = u_ref[c, plane, 7:8, :]
        out_ref[6 + plane : 7 + plane, :] = mod_ref[plane, 7:8, :]
        out_ref[8 + plane : 9 + plane, :] = phase_ref[plane, 7:8, :].astype(jnp.float32)
    out_ref[10:16, :] = jnp.zeros((6, out_ref.shape[1]), jnp.float32)


def fetch_kernel(u_hbm, load_hbm, mod_hbm, phase_hbm, u_ref, load_ref, mod_ref, phase_ref, sems):
    targets = (u_ref, load_ref, mod_ref, phase_ref)
    for copy in started((u_hbm, load_hbm, mod_hbm, phase_hbm), targets, sems):
        copy.wait()


def prepare_kernel(table, u_ref, load_ref, mod_ref, phase_ref, tiles_ref, back_ref, ahead_ref, work_ref):
    half, cols = u_ref.shape[2] // 2, u_ref.shape[3]
    quarter = half // 2
    fill_coefficients(table, tiles_ref)
    summer, rows = Summer(tiles_ref), Rows(work_ref)
    even_zero, odd_zero, top_zero = local_plane(rows, u_ref, None, 0)
    zero = plane_views(even_zero, odd_zero, top_zero)
    one = plane_views(*local_plane(rows, u_ref, None, 1))
    rows_zero = element_rows(rows, mod_ref, phase_ref, None, 0)
    rows_one = element_rows(rows, mod_ref, phase_ref, None, 1)
    even = even_lanes((half, cols))
    own, beyond = None, None
    for cy in range(2):
        elements = Elements(*rows_zero[cy])
        part = summer.force(
            elements, cy, terms_of(zero, 0, cy, 0, "o") + terms_of(one, 0, cy, 1, "so")
        )
        own = part if own is None else added(own, part)
        elements = Elements(*rows_one[cy])
        part = summer.force(elements, 2 + cy, terms_of(one, 1, cy, 0, "so"))
        beyond = part if beyond is None else added(beyond, part)
        for k in range(2):
            start = (6 + 2 * k + cy) * half
            back_ref[start : start + half, :] = rows_zero[cy][k]
            start = half + quarter + (2 * k + cy) * half
            ahead_ref[start : start + half, :] = rows_one[cy][k]
    own, beyond = at_nodes(own, cols), at_nodes(beyond, cols)
    back_ref[10 * half :, :] = jnp.zeros((8, cols), jnp.float32)
    for c in range(3):
        left = rows.split(load_ref[c, 0])[0] - own[c]
        back_ref[c * half : (c + 1) * half, :] = jnp.where(even, left, even_zero[c])
        back_ref[(3 + c) * half : (4 + c) * half, :] = odd_zero[c]
    ahead_ref[0:half, :] = jnp.where(even, beyond[0], last_lane(beyond[1]))
    ahead_ref[half : half + quarter, :] = jnp.where(
        even[:quarter], beyond[2][:quarter], last_lane(beyond[2][quarter:])
    )


def top_kernel(
    tiles_ref, u_ref, halo_ref, back_in, ahead_in, back_ref, ahead_ref, first_ref, second_ref
):
    half, cols = u_ref.shape[2] // 2, u_ref.shape[3]
    quarter = half // 2
    summer = Summer(tiles_ref)

    def wide(row):
        return jnp.broadcast_to(row, (8, cols))

    views, corners = [], []
    for plane in range(2):
        before = [wide(halo_ref[3 * plane + c : 3 * plane + c + 1, :]) for c in range(3)]
        same = [wide(u_ref[c, plane, 0:1, :]) for c in range(3)]
        views.append(([pair_even(a) for a in same], None, [pair_odd(a) for a in before]))
        corners.append(
            Elements(wide(halo_ref[6 + plane : 7 + plane, :]), wide(halo_ref[8 + plane : 9 + plane, :]))
        )
    own = summer.force(
        corners[0], 1, terms_of(views[0], 0, 1, 0, "o") + terms_of(views[1], 0, 1, 1, "so")
    )
    beyond = summer.force(corners[1], 3, terms_of(views[1], 1, 1, 0, "so"))
    own, beyond = at_nodes(own, cols), at_nodes(beyond, cols)
    even = even_lanes((1, cols))
    back_ref[...] = back_in[...]
    ahead_ref[...] = ahead_in[...]
    for c in range(3):
        old = back_in[c * half : c * half + 1, :]
        back_ref[c * half : c * half + 1, :] = jnp.where(even, old - own[c][0:1], old)
    back_ref[10 * half : 10 * half + 3, :] = halo_ref[0:3, :]
    for k in range(2):
        start = (7 + 2 * k) * half
        back_ref[start : start + 1, :] = halo_ref[6 + 2 * k : 7 + 2 * k, :]
        start = half + quarter + (2 * k + 1) * half
        ahead_ref[start : start + 1, :] = halo_ref[7 + 2 * k : 8 + 2 * k, :]
    ahead_ref[0:1, :] = ahead_in[0:1, :] + jnp.where(even, beyond[0][0:1], last_lane(beyond[1])[0:1])
    ahead_ref[half : half + 1, :] = jnp.where(
        even, ahead_in[half : half + 1, :] + beyond[2][0:1], ahead_in[half : half + 1, :]
    )
    first_ref[...] = back_ref[: first_ref.shape[0], :]
    second_ref[...] = back_ref[first_ref.shape[0] :, :]


def inner_kernel(tiles_ref, u_ref, load_ref, mod_ref, phase_ref, halo_ref, sums_ref, own_ref, work_ref):
    half, cols = u_ref.shape[2] // 2, u_ref.shape[3]
    summer, rows = Summer(tiles_ref), Rows(work_ref)
    zero = plane_views(*local_plane(rows, u_ref, halo_ref, 0))
    one = plane_views(*local_plane(rows, u_ref, halo_ref, 1))
    rows_zero = element_rows(rows, mod_ref, phase_ref, halo_ref, 0)
    rows_one = element_rows(rows, mod_ref, phase_ref, halo_ref, 1)
    weigh_own(
        summer, [[Elements(*pair) for pair in rows] for rows in (rows_zero, rows_one)], own_ref
    )
    total, middle, first, last = None, None, None, None
    for cy in range(2):
        left, right = Elements(*rows_zero[cy]), Elements(*rows_one[cy])
        part = summer.force(left, 2 + cy, terms_of(zero, 1, cy, 0, "o") + terms_of(one, 1, cy, 1, "o"))
        part = added(part, summer.force(right, cy, terms_of(one, 0, cy, 0, "o")))
        total = part if total is None else added(total, part)
        near = summer.diagonal(left, cy)
        mid = added(summer.diagonal(left, 2 + cy), summer.diagonal(right, cy))
        far = summer.diagonal(right, 2 + cy)
        first = near if first is None else added(first, near)
        middle = mid if middle is None else added(middle, mid)
        last = far if last is None else added(last, far)
    total = at_nodes(total, cols)
    for c in range(3):
        sums_ref[c] = rows.split(load_ref[c, 1])[0] - total[c]
    solved = inverse_of(at_nodes(middle, cols))
    first = at_nodes(first, cols)
    last = at_nodes(last, cols)
    for k in range(9):
        sums_ref[3 + k] = solved[k]
        sums_ref[12 + k] = first[k]
        sums_ref[21 + k] = last[k]


def unpacked(a, half):
    quarter = half // 2
    block = a[0:half, :]
    rest = a[half : half + quarter, :]
    return [block, next_lane(block), jnp.concatenate([rest, next_lane(rest)], axis=0)]


def far_kernel(tiles_ref, sums_ref, own_ref, mine_ahead, odd_ref, top_ref, end_ref, out_ref):
    half, cols = out_ref.shape[1:]
    summer = Summer(tiles_ref)
    back = jnp.concatenate([top_ref[...], end_ref[...]], axis=0) + odd_ref[...]
    even_two = [back[c * half : (c + 1) * half] for c in range(3)]
    odd_two = [back[(3 + c) * half : (4 + c) * half] for c in range(3)]
    top_two = [back[10 * half + c : 10 * half + c + 1] for c in range(3)]
    two = plane_views(even_two, odd_two, top_two)
    after, upper, beyond = None, None, None
    for cy in range(2):
        start = (6 + cy) * half
        plus = Elements(back[start : start + half], back[start + 2 * half : start + 3 * half])
        part = own_force(own_ref, 1, 2 + cy, terms_of(two, 1, cy, 1, "o"))
        after = part if after is None else added(after, part)
        part = own_force(own_ref, 1, cy, terms_of(two, 0, cy, 1, "o"))
        beyond = part if beyond is None else added(beyond, part)
        part = summer.diagonal(plus, cy)
        upper = part if upper is None else added(upper, part)
    after, upper = at_nodes(after, cols), at_nodes(upper, cols)
    sent = unpacked(mine_ahead, half)
    right = [even_two[c] - sent[c] - after[c] for c in range(3)]
    solved = applied(inverse_of([sums_ref[21 + k] + upper[k] for k in range(9)]), right)
    far = [pair_even(a)["s"] for a in solved]
    for cy in range(2):
        beyond = added(beyond, own_force(own_ref, 1, cy, [(2 + cy, "s", far)]))
    beyond = at_nodes(beyond, cols)
    for c in range(3):
        out_ref[c] = sums_ref[c] - beyond[c]


def near_kernel(
    tiles_ref, u_ref, halo_ref, sums_ref, own_ref, mine_back, ahead_ref, right_ref, out_ref, work_ref
):
    half, cols = u_ref.shape[2] // 2, u_ref.shape[3]
    quarter = half // 2
    summer, rows = Summer(tiles_ref), Rows(work_ref)
    even_zero, odd_zero, top_zero = local_plane(rows, u_ref, halo_ref, 0)
    zero = plane_views(even_zero, odd_zero, top_zero)
    even = even_lanes((half, cols))
    before, lower = None, None
    for cy in range(2):
        start = half + quarter + cy * half
        minus = Elements(ahead_ref[start : start + half, :], ahead_ref[start + 2 * half : start + 3 * half, :])
        part = summer.force(minus, 2 + cy, terms_of(zero, 1, cy, 1, "o"))
        before = part if before is None else added(before, part)
        part = summer.diagonal(minus, 2 + cy)
        lower = part if lower is None else added(lower, part)
    before, lower = at_nodes(before, cols), at_nodes(lower, cols)
    came = unpacked(ahead_ref, half)
    right = [mine_back[c * half : (c + 1) * half, :] - came[c] - before[c] for c in range(3)]
    first_new = applied(inverse_of([sums_ref[12 + k] + lower[k] for k in range(9)]), right)
    near = [pair_even(a)["s"] for a in first_new]
    beyond = own_force(own_ref, 0, 2, [(0, "s", near)])
    beyond = added(beyond, own_force(own_ref, 0, 3, [(1, "s", near)]))
    beyond = at_nodes(beyond, cols)
    inverse = [sums_ref[3 + k] for k in range(9)]
    second_new = applied(inverse, [right_ref[c] - beyond[c] for c in range(3)])
    for c in range(3):
        out_ref[c, 0] = rows.merge(jnp.where(even, first_new[c], even_zero[c]), odd_zero[c])
        own, other = rows.split(u_ref[c, 1])
        out_ref[c, 1] = rows.merge(jnp.where(even, second_new[c], own), other)


def whole():
    return pl.BlockSpec(memory_space=pltpu.VMEM)


def scalars():
    return pl.BlockSpec(memory_space=pltpu.SMEM)


def on_device(displacement, load, element_phase, element_modulus, stiffness):
    planes, rows, cols = displacement.shape[1:]
    half = rows // 2
    kind = displacement.dtype
    table = stiffness.reshape(-1)
    slots = 16
    hbm = [
        pltpu.with_memory_space_constraint(a, pltpu.HBM)
        for a in (displacement, load, element_modulus, element_phase)
    ]
    rim = pl.pallas_call(
        rim_kernel,
        in_specs=[pl.BlockSpec(memory_space=pltpu.HBM)] * 3,
        out_specs=whole(),
        out_shape=jax.ShapeDtypeStruct((16, cols), kind),
        scratch_shapes=[
            pltpu.VMEM((3, planes, 8, cols), kind),
            pltpu.VMEM((planes, 8, cols), kind),
            pltpu.VMEM((planes, 8, cols), element_phase.dtype),
            pltpu.SemaphoreType.DMA((3,)),
        ],
        compiler_params=pltpu.CompilerParams(vmem_limit_bytes=8 << 20),
    )(hbm[0], hbm[2], hbm[3])
    displacement, load, element_modulus, element_phase = pl.pallas_call(
        fetch_kernel,
        in_specs=[pl.BlockSpec(memory_space=pltpu.HBM)] * 4,
        out_specs=[whole()] * 4,
        out_shape=[jax.ShapeDtypeStruct(a.shape, a.dtype) for a in hbm],
        scratch_shapes=[pltpu.SemaphoreType.DMA((4,))],
        compiler_params=pltpu.CompilerParams(vmem_limit_bytes=8 << 20),
        cost_estimate=pl.CostEstimate(flops=1_000_000_000, bytes_accessed=0, transcendentals=0),
    )(*hbm)
    halo = shifted(rim, "gy", 1)
    back_rows, ahead_rows = 10 * half + 8, 5 * half + half // 2
    params = pltpu.CompilerParams(vmem_limit_bytes=24 << 20)
    scratch = [pltpu.VMEM((slots, cols // 128, rows, 128), kind)]
    ahead_shape = jax.ShapeDtypeStruct((ahead_rows, cols), kind)
    back_shape = jax.ShapeDtypeStruct((back_rows, cols), kind)
    part_shape = jax.ShapeDtypeStruct((back_rows // 2, cols), kind)
    tile_shape = jax.ShapeDtypeStruct((3 * PHASE_ROWS, 8, 128), kind)
    coefficients, back, ahead = pl.pallas_call(
        prepare_kernel,
        in_specs=[scalars()] + [whole()] * 4,
        out_specs=[whole()] * 3,
        out_shape=[tile_shape, back_shape, ahead_shape],
        scratch_shapes=scratch,
        compiler_params=params,
        cost_estimate=pl.CostEstimate(flops=20_000_000, bytes_accessed=6_000_000, transcendentals=0),
    )(table, displacement, load, element_modulus, element_phase)
    back, ahead, top, end = pl.pallas_call(
        top_kernel,
        in_specs=[whole()] * 5,
        out_specs=[whole()] * 4,
        out_shape=[back_shape, ahead_shape, part_shape, part_shape],
        compiler_params=params,
    )(coefficients, displacement, halo, back, ahead)
    from_odd = shifted_from(back, "gx", -1, 1)
    from_last = shifted(ahead, "gx", 1)
    from_even = [shifted_from(part, "gx", -1, 0) for part in (top, end)]
    sums, own = pl.pallas_call(
        inner_kernel,
        in_specs=[whole()] * 6,
        out_specs=[whole()] * 2,
        out_shape=[
            jax.ShapeDtypeStruct((30, half, cols), kind),
            jax.ShapeDtypeStruct((9 * len(OWN_TERMS), half * cols // 1024, 8, 128), kind),
        ],
        scratch_shapes=scratch,
        compiler_params=params,
        cost_estimate=pl.CostEstimate(flops=20_000_000, bytes_accessed=1_000_000, transcendentals=0),
    )(coefficients, displacement, load, element_modulus, element_phase, halo)
    right = pl.pallas_call(
        far_kernel,
        in_specs=[whole()] * 7,
        out_specs=whole(),
        out_shape=jax.ShapeDtypeStruct((3, half, cols), kind),
        compiler_params=params,
    )(coefficients, sums, own, ahead, from_odd, *from_even)
    return pl.pallas_call(
        near_kernel,
        in_specs=[whole()] * 8,
        out_specs=whole(),
        out_shape=jax.ShapeDtypeStruct(displacement.shape, kind),
        scratch_shapes=scratch,
        compiler_params=params,
    )(coefficients, displacement, halo, sums, own, back, from_last, right)


def solution(mesh):
    in_specs = (
        P(None, "gx", "gy", None),
        P(None, "gx", "gy", None),
        P("gx", "gy", None),
        P("gx", "gy", None),
        P(),
    )
    out_specs = P(None, "gx", "gy", None)
    return jax.shard_map(
        on_device, mesh=mesh, in_specs=in_specs, out_specs=out_specs, check_vma=False
    )
```

```python
import jax
import jax.numpy as jnp
from jax import lax
from jax.experimental import pallas as pl
from jax.experimental.pallas import tpu as pltpu
from jax.sharding import PartitionSpec as P

PARITY = {"0": (0, 0), "1": (1, 1), "s": (0, 1), "o": (1, 0)}


def shifted(x, axis, by):
    devices = lax.axis_size(axis)
    return lax.ppermute(x, axis, [(i, (i + by) % devices) for i in range(devices)])


def shifted_from(x, axis, by, parity):
    devices = lax.axis_size(axis)
    return lax.ppermute(x, axis, [(i, (i + by) % devices) for i in range(parity, devices, 2)])


def tiles(a):
    rows, cols = a.shape
    return jnp.stack(
        [a[r : r + 8, c : c + 128] for r in range(0, rows, 8) for c in range(0, cols, 128)]
    )


def flat(t, cols):
    across = cols // 128
    rows = [
        jnp.concatenate([t[r + c] for c in range(across)], axis=1)
        for r in range(0, t.shape[0], across)
    ]
    return jnp.concatenate(rows, axis=0)


def even_lanes(shape):
    return lax.broadcasted_iota(jnp.int32, shape, len(shape) - 1) % 2 == 0


def next_lane(a):
    return pltpu.roll(a, a.shape[-1] - 1, a.ndim - 1)


def last_lane(a):
    return pltpu.roll(a, 1, a.ndim - 1)


def down_row(a, top):
    first = lax.broadcasted_iota(jnp.int32, a.shape, 0) == 0
    return jnp.where(first, jnp.broadcast_to(top, a.shape), pltpu.roll(a, 1, 0))


def pair_even(a):
    here, there = tiles(a), tiles(next_lane(a))
    even = even_lanes((8, 128))[None]
    return {"s": jnp.where(even, here, there), "o": jnp.where(even, there, here)}


def pair_odd(a):
    return {"0": tiles(a), "1": tiles(next_lane(a))}


def plane_views(even_rows, odd_rows, tops):
    same = [pair_even(a) for a in even_rows]
    after = [pair_odd(a) for a in odd_rows]
    before = [pair_odd(down_row(a, top)) for a, top in zip(odd_rows, tops)]
    return same, after, before


class Elements:
    def __init__(self, modulus, phase):
        phase = tiles(phase)
        self.modulus, self.first, self.second = tiles(modulus), phase == 0, phase == 1


def coefficient(corner, partner, kind, i, j):
    return ((corner * 4 + partner) * 2 + ("0s1o".index(kind) // 2)) * 9 + i * 3 + j


PHASE_ROWS = 4 * 4 * 2 * 9


def fill_coefficients(table, tiles_ref):
    even = even_lanes((8, 128))
    for ph in range(3):
        for corner in range(4):
            for partner in range(4):
                for kind in "so" if partner % 2 == corner % 2 else "01":
                    for i in range(3):
                        for j in range(3):
                            places = [
                                table[(((ph * 8 + corner * 2 + parity) * 8 + partner * 2 + side) * 3 + i) * 3 + j]
                                for parity, side in enumerate(PARITY[kind])
                            ]
                            row = ph * PHASE_ROWS + coefficient(corner, partner, kind, i, j)
                            tiles_ref[row] = jnp.where(even, places[0], places[1])


class Summer:
    def __init__(self, tiles_ref):
        self.tiles = tiles_ref

    def entry(self, elements, corner, partner, kind, i, j):
        row = coefficient(corner, partner, kind, i, j)
        picked = [self.tiles[ph * PHASE_ROWS + row][None] for ph in range(3)]
        return jnp.where(elements.first, picked[0], jnp.where(elements.second, picked[1], picked[2]))

    def force(self, elements, corner, terms):
        total = [None] * 3
        for partner, kind, values in terms:
            for i in range(3):
                for j in range(3):
                    part = self.entry(elements, corner, partner, kind, i, j) * values[j]
                    total[i] = part if total[i] is None else total[i] + part
        return [elements.modulus * part for part in total]

    def diagonal(self, elements, corner):
        return [
            elements.modulus * self.entry(elements, corner, corner, "s", i, j)
            for i in range(3)
            for j in range(3)
        ]


def pick(views, kind):
    return [view[kind] for view in views]


def terms_of(views, cx, cy, dx, kinds):
    same, after, before = views
    other = after if cy == 0 else before
    found = [(dx * 2 + cy, kind, pick(same, kind)) for kind in kinds]
    found += [(dx * 2 + 1 - cy, kind, pick(other, kind)) for kind in ("0", "1")]
    return found


OWN_TERMS = [
    (cx, corner, partner, kind)
    for cy in range(2)
    for cx, corner, partners in ((0, 2 + cy, ((cy, "s"),)), (1, cy, None), (1, 2 + cy, None))
    for partner, kind in (
        partners
        or (
            ([(2 + cy, "s")] if corner < 2 else [])
            + [(2 + cy, "o"), (3 - cy, "0"), (3 - cy, "1")]
        )
    )
]


def weigh_own(summer, elements, own_ref):
    for place, (plane, corner, partner, kind) in enumerate(OWN_TERMS):
        part = elements[plane][corner % 2]
        for i in range(3):
            for j in range(3):
                own_ref[place * 9 + i * 3 + j] = part.modulus * summer.entry(part, corner, partner, kind, i, j)


def own_force(own_ref, plane, corner, terms):
    total = [None] * 3
    for partner, kind, values in terms:
        place = OWN_TERMS.index((plane, corner, partner, kind))
        for i in range(3):
            for j in range(3):
                part = own_ref[place * 9 + i * 3 + j] * values[j]
                total[i] = part if total[i] is None else total[i] + part
    return total


def added(left, right):
    return [a + b for a, b in zip(left, right)]


def at_nodes(parts, cols):
    out = []
    for part in parts:
        whole = flat(part, cols)
        out.append(whole + last_lane(whole))
    return out


def inverse_of(m):
    m00, m01, m02, m10, m11, m12, m20, m21, m22 = m
    c00 = m11 * m22 - m12 * m21
    c01 = m12 * m20 - m10 * m22
    c02 = m10 * m21 - m11 * m20
    c10 = m02 * m21 - m01 * m22
    c11 = m00 * m22 - m02 * m20
    c12 = m01 * m20 - m00 * m21
    c20 = m01 * m12 - m02 * m11
    c21 = m02 * m10 - m00 * m12
    c22 = m00 * m11 - m01 * m10
    determinant = m00 * c00 + m01 * c01 + m02 * c02
    scale = 1.0 / determinant
    return [a * scale for a in (c00, c10, c20, c01, c11, c21, c02, c12, c22)]


def applied(inverse, right):
    return [sum(inverse[3 * i + j] * right[j] for j in range(3)) for i in range(3)]


class Rows:
    def __init__(self, work_ref):
        self.work, self.slot = work_ref, 0

    def split(self, a):
        parts, slot, half = a.shape[1] // 128, self.slot, a.shape[0] // 2
        self.slot += 1
        for k in range(parts):
            self.work[slot, k] = a[:, k * 128 : (k + 1) * 128]
        return tuple(
            jnp.concatenate([self.work[slot, k, pl.ds(bit, half, 2), :] for k in range(parts)], axis=1)
            for bit in range(2)
        )

    def merge(self, even, odd):
        parts, slot, half = even.shape[1] // 128, self.slot, even.shape[0]
        self.slot += 1
        for k in range(parts):
            self.work[slot, k, pl.ds(0, half, 2), :] = even[:, k * 128 : (k + 1) * 128]
            self.work[slot, k, pl.ds(1, half, 2), :] = odd[:, k * 128 : (k + 1) * 128]
        return jnp.concatenate([self.work[slot, k] for k in range(parts)], axis=1)


def halo_row(halo_ref, row, cols):
    return jnp.zeros((1, cols), jnp.float32) if halo_ref is None else halo_ref[row : row + 1, :]


def local_plane(rows, u_ref, halo_ref, plane):
    split = [rows.split(u_ref[c, plane]) for c in range(3)]
    even, odd = [a for a, _ in split], [b for _, b in split]
    tops = [halo_row(halo_ref, 3 * plane + c, u_ref.shape[-1]) for c in range(3)]
    return even, odd, tops


def element_rows(rows, mod_ref, phase_ref, halo_ref, plane):
    split = [rows.split(mod_ref[plane]), rows.split(phase_ref[plane].astype(jnp.float32))]
    even, odd = [a for a, _ in split], [b for _, b in split]
    before = (
        down_row(odd[0], halo_row(halo_ref, 6 + plane, mod_ref.shape[-1])),
        down_row(odd[1], halo_row(halo_ref, 8 + plane, mod_ref.shape[-1])),
    )
    return even, before


def started(sources, targets, sems):
    copies = [
        pltpu.make_async_copy(source, target, sems.at[k])
        for k, (source, target) in enumerate(zip(sources, targets))
    ]
    for copy in copies:
        copy.start()
    return copies


def rim_kernel(u_hbm, mod_hbm, phase_hbm, out_ref, u_ref, mod_ref, phase_ref, sems):
    edge = pl.ds(u_hbm.shape[2] - 8, 8)
    sources = (u_hbm.at[:, :, edge, :], mod_hbm.at[:, edge, :], phase_hbm.at[:, edge, :])
    for copy in started(sources, (u_ref, mod_ref, phase_ref), sems):
        copy.wait()
    for plane in range(2):
        for c in range(3):
            out_ref[3 * plane + c : 3 * plane + c + 1, :] = u_ref[c, plane, 7:8, :]
        out_ref[6 + plane : 7 + plane, :] = mod_ref[plane, 7:8, :]
        out_ref[8 + plane : 9 + plane, :] = phase_ref[plane, 7:8, :].astype(jnp.float32)
    out_ref[10:16, :] = jnp.zeros((6, out_ref.shape[1]), jnp.float32)


def fetch_kernel(u_hbm, load_hbm, mod_hbm, phase_hbm, u_ref, load_ref, mod_ref, phase_ref, sems):
    targets = (u_ref, load_ref, mod_ref, phase_ref)
    for copy in started((u_hbm, load_hbm, mod_hbm, phase_hbm), targets, sems):
        copy.wait()


def prepare_kernel(table, u_ref, load_ref, mod_ref, phase_ref, tiles_ref, back_ref, ahead_ref, work_ref):
    half, cols = u_ref.shape[2] // 2, u_ref.shape[3]
    quarter = half // 2
    fill_coefficients(table, tiles_ref)
    summer, rows = Summer(tiles_ref), Rows(work_ref)
    even_zero, odd_zero, top_zero = local_plane(rows, u_ref, None, 0)
    zero = plane_views(even_zero, odd_zero, top_zero)
    one = plane_views(*local_plane(rows, u_ref, None, 1))
    rows_zero = element_rows(rows, mod_ref, phase_ref, None, 0)
    rows_one = element_rows(rows, mod_ref, phase_ref, None, 1)
    even = even_lanes((half, cols))
    own, beyond = None, None
    for cy in range(2):
        elements = Elements(*rows_zero[cy])
        part = summer.force(
            elements, cy, terms_of(zero, 0, cy, 0, "o") + terms_of(one, 0, cy, 1, "so")
        )
        own = part if own is None else added(own, part)
        elements = Elements(*rows_one[cy])
        part = summer.force(elements, 2 + cy, terms_of(one, 1, cy, 0, "so"))
        beyond = part if beyond is None else added(beyond, part)
        for k in range(2):
            start = (6 + 2 * k + cy) * half
            back_ref[start : start + half, :] = rows_zero[cy][k]
            start = half + quarter + (2 * k + cy) * half
            ahead_ref[start : start + half, :] = rows_one[cy][k]
    own, beyond = at_nodes(own, cols), at_nodes(beyond, cols)
    back_ref[10 * half :, :] = jnp.zeros((8, cols), jnp.float32)
    for c in range(3):
        left = rows.split(load_ref[c, 0])[0] - own[c]
        back_ref[c * half : (c + 1) * half, :] = jnp.where(even, left, even_zero[c])
        back_ref[(3 + c) * half : (4 + c) * half, :] = odd_zero[c]
    ahead_ref[0:half, :] = jnp.where(even, beyond[0], last_lane(beyond[1]))
    ahead_ref[half : half + quarter, :] = jnp.where(
        even[:quarter], beyond[2][:quarter], last_lane(beyond[2][quarter:])
    )


def top_kernel(
    tiles_ref, u_ref, halo_ref, back_in, ahead_in, back_ref, ahead_ref, first_ref, second_ref
):
    half, cols = u_ref.shape[2] // 2, u_ref.shape[3]
    quarter = half // 2
    summer = Summer(tiles_ref)

    def wide(row):
        return jnp.broadcast_to(row, (8, cols))

    views, corners = [], []
    for plane in range(2):
        before = [wide(halo_ref[3 * plane + c : 3 * plane + c + 1, :]) for c in range(3)]
        same = [wide(u_ref[c, plane, 0:1, :]) for c in range(3)]
        views.append(([pair_even(a) for a in same], None, [pair_odd(a) for a in before]))
        corners.append(
            Elements(wide(halo_ref[6 + plane : 7 + plane, :]), wide(halo_ref[8 + plane : 9 + plane, :]))
        )
    own = summer.force(
        corners[0], 1, terms_of(views[0], 0, 1, 0, "o") + terms_of(views[1], 0, 1, 1, "so")
    )
    beyond = summer.force(corners[1], 3, terms_of(views[1], 1, 1, 0, "so"))
    own, beyond = at_nodes(own, cols), at_nodes(beyond, cols)
    even = even_lanes((1, cols))
    back_ref[...] = back_in[...]
    ahead_ref[...] = ahead_in[...]
    for c in range(3):
        old = back_in[c * half : c * half + 1, :]
        back_ref[c * half : c * half + 1, :] = jnp.where(even, old - own[c][0:1], old)
    back_ref[10 * half : 10 * half + 3, :] = halo_ref[0:3, :]
    for k in range(2):
        start = (7 + 2 * k) * half
        back_ref[start : start + 1, :] = halo_ref[6 + 2 * k : 7 + 2 * k, :]
        start = half + quarter + (2 * k + 1) * half
        ahead_ref[start : start + 1, :] = halo_ref[7 + 2 * k : 8 + 2 * k, :]
    ahead_ref[0:1, :] = ahead_in[0:1, :] + jnp.where(even, beyond[0][0:1], last_lane(beyond[1])[0:1])
    ahead_ref[half : half + 1, :] = jnp.where(
        even, ahead_in[half : half + 1, :] + beyond[2][0:1], ahead_in[half : half + 1, :]
    )
    first_ref[...] = back_ref[: first_ref.shape[0], :]
    cut = first_ref.shape[0]
    second_ref[...] = back_ref[cut : cut + second_ref.shape[0], :]


def inner_kernel(tiles_ref, u_ref, load_ref, mod_ref, phase_ref, halo_ref, sums_ref, own_ref, work_ref):
    half, cols = u_ref.shape[2] // 2, u_ref.shape[3]
    summer, rows = Summer(tiles_ref), Rows(work_ref)
    zero = plane_views(*local_plane(rows, u_ref, halo_ref, 0))
    one = plane_views(*local_plane(rows, u_ref, halo_ref, 1))
    rows_zero = element_rows(rows, mod_ref, phase_ref, halo_ref, 0)
    rows_one = element_rows(rows, mod_ref, phase_ref, halo_ref, 1)
    weigh_own(
        summer, [[Elements(*pair) for pair in rows] for rows in (rows_zero, rows_one)], own_ref
    )
    total, middle, first, last = None, None, None, None
    for cy in range(2):
        left, right = Elements(*rows_zero[cy]), Elements(*rows_one[cy])
        part = summer.force(left, 2 + cy, terms_of(zero, 1, cy, 0, "o") + terms_of(one, 1, cy, 1, "o"))
        part = added(part, summer.force(right, cy, terms_of(one, 0, cy, 0, "o")))
        total = part if total is None else added(total, part)
        near = summer.diagonal(left, cy)
        mid = added(summer.diagonal(left, 2 + cy), summer.diagonal(right, cy))
        far = summer.diagonal(right, 2 + cy)
        first = near if first is None else added(first, near)
        middle = mid if middle is None else added(middle, mid)
        last = far if last is None else added(last, far)
    total = at_nodes(total, cols)
    for c in range(3):
        sums_ref[c] = rows.split(load_ref[c, 1])[0] - total[c]
    solved = inverse_of(at_nodes(middle, cols))
    first = at_nodes(first, cols)
    last = at_nodes(last, cols)
    for k in range(9):
        sums_ref[3 + k] = solved[k]
        sums_ref[12 + k] = first[k]
        sums_ref[21 + k] = last[k]


def unpacked(a, half):
    quarter = half // 2
    block = a[0:half, :]
    rest = a[half : half + quarter, :]
    return [block, next_lane(block), jnp.concatenate([rest, next_lane(rest)], axis=0)]


def far_kernel(tiles_ref, sums_ref, own_ref, mine_ahead, odd_ref, top_ref, end_ref, out_ref):
    half, cols = out_ref.shape[1:]
    summer = Summer(tiles_ref)
    back = jnp.concatenate([top_ref[...], end_ref[...]], axis=0)
    back = back + odd_ref[: back.shape[0], :]
    even_two = [back[c * half : (c + 1) * half] for c in range(3)]
    odd_two = [back[(3 + c) * half : (4 + c) * half] for c in range(3)]
    top_two = [back[10 * half + c : 10 * half + c + 1] for c in range(3)]
    two = plane_views(even_two, odd_two, top_two)
    after, upper, beyond = None, None, None
    for cy in range(2):
        start = (6 + cy) * half
        plus = Elements(back[start : start + half], back[start + 2 * half : start + 3 * half])
        part = own_force(own_ref, 1, 2 + cy, terms_of(two, 1, cy, 1, "o"))
        after = part if after is None else added(after, part)
        part = own_force(own_ref, 1, cy, terms_of(two, 0, cy, 1, "o"))
        beyond = part if beyond is None else added(beyond, part)
        part = summer.diagonal(plus, cy)
        upper = part if upper is None else added(upper, part)
    after, upper = at_nodes(after, cols), at_nodes(upper, cols)
    sent = unpacked(mine_ahead, half)
    right = [even_two[c] - sent[c] - after[c] for c in range(3)]
    solved = applied(inverse_of([sums_ref[21 + k] + upper[k] for k in range(9)]), right)
    far = [pair_even(a)["s"] for a in solved]
    for cy in range(2):
        beyond = added(beyond, own_force(own_ref, 1, cy, [(2 + cy, "s", far)]))
    beyond = at_nodes(beyond, cols)
    for c in range(3):
        out_ref[c] = sums_ref[c] - beyond[c]


def near_kernel(
    tiles_ref, u_ref, halo_ref, sums_ref, own_ref, mine_back, ahead_ref, right_ref, out_ref, work_ref
):
    half, cols = u_ref.shape[2] // 2, u_ref.shape[3]
    quarter = half // 2
    summer, rows = Summer(tiles_ref), Rows(work_ref)
    even_zero, odd_zero, top_zero = local_plane(rows, u_ref, halo_ref, 0)
    zero = plane_views(even_zero, odd_zero, top_zero)
    even = even_lanes((half, cols))
    before, lower = None, None
    for cy in range(2):
        start = half + quarter + cy * half
        minus = Elements(ahead_ref[start : start + half, :], ahead_ref[start + 2 * half : start + 3 * half, :])
        part = summer.force(minus, 2 + cy, terms_of(zero, 1, cy, 1, "o"))
        before = part if before is None else added(before, part)
        part = summer.diagonal(minus, 2 + cy)
        lower = part if lower is None else added(lower, part)
    before, lower = at_nodes(before, cols), at_nodes(lower, cols)
    came = unpacked(ahead_ref, half)
    right = [mine_back[c * half : (c + 1) * half, :] - came[c] - before[c] for c in range(3)]
    first_new = applied(inverse_of([sums_ref[12 + k] + lower[k] for k in range(9)]), right)
    near = [pair_even(a)["s"] for a in first_new]
    beyond = own_force(own_ref, 0, 2, [(0, "s", near)])
    beyond = added(beyond, own_force(own_ref, 0, 3, [(1, "s", near)]))
    beyond = at_nodes(beyond, cols)
    inverse = [sums_ref[3 + k] for k in range(9)]
    second_new = applied(inverse, [right_ref[c] - beyond[c] for c in range(3)])
    for c in range(3):
        out_ref[c, 0] = rows.merge(jnp.where(even, first_new[c], even_zero[c]), odd_zero[c])
        own, other = rows.split(u_ref[c, 1])
        out_ref[c, 1] = rows.merge(jnp.where(even, second_new[c], own), other)


def whole():
    return pl.BlockSpec(memory_space=pltpu.VMEM)


def scalars():
    return pl.BlockSpec(memory_space=pltpu.SMEM)


def on_device(displacement, load, element_phase, element_modulus, stiffness):
    planes, rows, cols = displacement.shape[1:]
    half = rows // 2
    kind = displacement.dtype
    table = stiffness.reshape(-1)
    slots = 16
    hbm = [
        pltpu.with_memory_space_constraint(a, pltpu.HBM)
        for a in (displacement, load, element_modulus, element_phase)
    ]
    rim = pl.pallas_call(
        rim_kernel,
        in_specs=[pl.BlockSpec(memory_space=pltpu.HBM)] * 3,
        out_specs=whole(),
        out_shape=jax.ShapeDtypeStruct((16, cols), kind),
        scratch_shapes=[
            pltpu.VMEM((3, planes, 8, cols), kind),
            pltpu.VMEM((planes, 8, cols), kind),
            pltpu.VMEM((planes, 8, cols), element_phase.dtype),
            pltpu.SemaphoreType.DMA((3,)),
        ],
        compiler_params=pltpu.CompilerParams(vmem_limit_bytes=8 << 20),
    )(hbm[0], hbm[2], hbm[3])
    displacement, load, element_modulus, element_phase = pl.pallas_call(
        fetch_kernel,
        in_specs=[pl.BlockSpec(memory_space=pltpu.HBM)] * 4,
        out_specs=[whole()] * 4,
        out_shape=[jax.ShapeDtypeStruct(a.shape, a.dtype) for a in hbm],
        scratch_shapes=[pltpu.SemaphoreType.DMA((4,))],
        compiler_params=pltpu.CompilerParams(vmem_limit_bytes=8 << 20),
        cost_estimate=pl.CostEstimate(flops=1_000_000_000, bytes_accessed=0, transcendentals=0),
    )(*hbm)
    halo = shifted(rim, "gy", 1)
    back_rows, ahead_rows = 10 * half + 8, 5 * half + half // 2
    params = pltpu.CompilerParams(vmem_limit_bytes=24 << 20)
    scratch = [pltpu.VMEM((slots, cols // 128, rows, 128), kind)]
    ahead_shape = jax.ShapeDtypeStruct((ahead_rows, cols), kind)
    back_shape = jax.ShapeDtypeStruct((back_rows, cols), kind)
    part_shapes = [jax.ShapeDtypeStruct((5 * half + k, cols), kind) for k in (0, 4)]
    tile_shape = jax.ShapeDtypeStruct((3 * PHASE_ROWS, 8, 128), kind)
    coefficients, back, ahead = pl.pallas_call(
        prepare_kernel,
        in_specs=[scalars()] + [whole()] * 4,
        out_specs=[whole()] * 3,
        out_shape=[tile_shape, back_shape, ahead_shape],
        scratch_shapes=scratch,
        compiler_params=params,
        cost_estimate=pl.CostEstimate(flops=20_000_000, bytes_accessed=6_000_000, transcendentals=0),
    )(table, displacement, load, element_modulus, element_phase)
    back, ahead, top, end = pl.pallas_call(
        top_kernel,
        in_specs=[whole()] * 5,
        out_specs=[whole()] * 4,
        out_shape=[back_shape, ahead_shape, *part_shapes],
        compiler_params=params,
    )(coefficients, displacement, halo, back, ahead)
    from_odd = shifted_from(back, "gx", -1, 1)
    from_last = shifted(ahead, "gx", 1)
    from_even = [shifted_from(part, "gx", -1, 0) for part in (top, end)]
    sums, own = pl.pallas_call(
        inner_kernel,
        in_specs=[whole()] * 6,
        out_specs=[whole()] * 2,
        out_shape=[
            jax.ShapeDtypeStruct((30, half, cols), kind),
            jax.ShapeDtypeStruct((9 * len(OWN_TERMS), half * cols // 1024, 8, 128), kind),
        ],
        scratch_shapes=scratch,
        compiler_params=params,
        cost_estimate=pl.CostEstimate(flops=20_000_000, bytes_accessed=1_000_000, transcendentals=0),
    )(coefficients, displacement, load, element_modulus, element_phase, halo)
    right = pl.pallas_call(
        far_kernel,
        in_specs=[whole()] * 7,
        out_specs=whole(),
        out_shape=jax.ShapeDtypeStruct((3, half, cols), kind),
        compiler_params=params,
    )(coefficients, sums, own, ahead, from_odd, *from_even)
    return pl.pallas_call(
        near_kernel,
        in_specs=[whole()] * 8,
        out_specs=whole(),
        out_shape=jax.ShapeDtypeStruct(displacement.shape, kind),
        scratch_shapes=scratch,
        compiler_params=params,
    )(coefficients, displacement, halo, sums, own, back, from_last, right)


def solution(mesh):
    in_specs = (
        P(None, "gx", "gy", None),
        P(None, "gx", "gy", None),
        P("gx", "gy", None),
        P("gx", "gy", None),
        P(),
    )
    out_specs = P(None, "gx", "gy", None)
    return jax.shard_map(
        on_device, mesh=mesh, in_specs=in_specs, out_specs=out_specs, check_vma=False
    )
```
